128 devices in a mesh: sec: 64 (over y, z, x), mpo: 2 (over core).
Axes of the slice: x: 4, y: 4, z: 4, core: 2. Of those that a mesh axis runs over, the one named last changes fastest.
Arguments:
- sector_dims: int32 [3072], P('sec'), may hold values from 1 to 256, 688128 in all
- new_owner: int32 [3072], P('sec'), may hold values from 0 to 63, as said below
- new_slot: int32 [3072], P('sec'), may hold values from 0 to 47, as said below
- block_pairs: int32 [3072, 4], P('sec', 'mpo'), may hold values from 0 to 47
- theta_blocks: bfloat16 [3072, 256, 256], P('sec'), may hold values from -6 to 6
- left_env: bfloat16 [3072, 4, 256, 256], P('sec', 'mpo'), may hold values from -0.1875 to 0.1875
- right_env: bfloat16 [4, 256, 256], P('mpo'), may hold values from -0.375 to 0.375
Outputs:
- applied: bfloat16 [256, 3072, 256], P('mpo', 'sec')
The draws below stay inside these ranges and needn't reach their ends.
Inputs may be any that keep to these rules, and one draw needn't show every extreme that they name: Rows 0 to sector_dims - 1 of a block are live; the largest equals 256. `new_owner`: every index of sec receives exactly 48 blocks; one index sends at most 1 block to any one index, and exactly 1 to some. `new_slot`: the blocks that one index receives take its 48 slots once each. `block_pairs`: partners are slots of the same index of sec as the block.
All inputs are finite; a program needn't handle non-finite values.
Results may differ from the reference program's by a relative error of at most 0.0049.
Values may be sent and summed in bfloat16 or wider, within the bound.
No kernel may reach another device: no remote copies, remote signals or barrier semaphores. Data moves between devices by JAX's collectives and lax.ppermute only.
A program may use at most 192 MiB of HBM per device.

```python
import math
import jax
import jax.numpy as jnp
import numpy as np
from jax import lax

TILE = 256
WB = 4
SLOTS = 48
NBLK = 3072
N_SEC = 64


def owner_tables(key):
    keys = jax.random.split(key, 4)
    per_peer = (SLOTS + N_SEC - 1) // N_SEC
    offsets = (jax.random.permutation(keys[0], N_SEC * per_peer) % N_SEC)[:SLOTS]
    first_perm = jax.random.permutation(keys[1], N_SEC)
    second_perm = jax.random.permutation(keys[2], N_SEC)
    places = jax.vmap(lambda sub_key: jax.random.permutation(sub_key, SLOTS))(jax.random.split(keys[3], N_SEC))
    source = jnp.arange(NBLK, dtype=jnp.int32) // SLOTS
    local_slot = jnp.arange(NBLK, dtype=jnp.int32) % SLOTS
    target = second_perm[(first_perm[source] + offsets[local_slot]) % N_SEC]
    return (target.astype(jnp.int32), places[target, local_slot].astype(jnp.int32))


def draw_new_owner(key, part):
    target, placed = owner_tables(key)
    return target


def draw_new_slot(key, part):
    target, placed = owner_tables(key)
    return placed


def plant(result, rng, low, high):
    longest = result.shape.index(max(result.shape))
    spots = []
    for shift in (0, 1):
        where = [jax.random.randint(jax.random.fold_in(rng, axis), (), 0, length) for axis, length in enumerate(result.shape)]
        where[longest] = (where[longest] + shift) % result.shape[longest]
        spots.append(tuple(where))
    return result.at[spots[0]].set(low).at[spots[1]].set(high)


def block_levels(stream_key, shape, cuts, least, largest):
    factor_of, own = 1.0, jax.random.fold_in(stream_key, 6)
    for axis_at, blocks in cuts:
        draws = jnp.exp(jax.random.uniform(jax.random.fold_in(own, axis_at), (blocks,), jnp.float32, least / len(cuts), largest / len(cuts)))
        factor_of = factor_of * jnp.repeat(draws, shape[axis_at] // blocks).reshape([-1 if axis == axis_at else 1 for axis in range(len(shape))])
    return factor_of


def profile(amount, total, bound, lean):
    portions = [(1 << 20) // math.isqrt(standing ** lean) + 1 for standing in range(2, amount + 1)]
    surplus, holding = total - bound - (amount - 1), [1] * (amount - 1)
    while surplus > 0:
        free = [i for i in range(amount - 1) if holding[i] < bound]
        mass, remaining = sum([portions[i] for i in free]), surplus
        for i in free:
            more = min(bound - holding[i], max(1, remaining * portions[i] // mass), surplus)
            holding[i] = holding[i] + more
            surplus = surplus - more
    return np.array([bound] + holding)


def uneven_parts(rng, amount, total, most, skew):
    if amount == 2:
        one = jax.random.randint(rng, (), max(1, total - most), min(most, total - 1) + 1)
        return jnp.stack([one, total - one])
    sizes = jnp.asarray(profile(amount, total, most, skew), jnp.int32)
    twos = (amount - 1) // 2
    source_of, taker = sizes[1:1 + 2 * twos:2], sizes[2:2 + 2 * twos:2]
    slack = jnp.minimum(source_of - 1, most - taker)
    moved = jax.random.randint(jax.random.fold_in(rng, 1), (twos,), 0, 1 << 20) % (slack + 1)
    sizes = sizes.at[1:1 + 2 * twos:2].set(source_of - moved).at[2:2 + 2 * twos:2].set(taker + moved)
    return sizes[jax.random.permutation(jax.random.fold_in(rng, 2), amount)]


def centred(own_key, extent, width, limit, cuts=(), held_as=jnp.bfloat16):
    entries = jax.random.normal(own_key, extent, jnp.float32) * width
    if len(cuts) > 0:
        entries = block_levels(own_key, extent, cuts, -0.22, 0.18) * entries
    return jnp.clip(entries, min=-limit, max=limit).astype(held_as)


def setup_inputs(seed: int = 0) -> dict:
    streams_of = jax.random.split(jax.random.key(seed), 8)
    sector_dims = uneven_parts(streams_of[0], NBLK, 7 * NBLK * TILE // 8, TILE, 2).astype(jnp.int32)
    new_owner = draw_new_owner(jax.random.fold_in(streams_of[7], 71), 0)
    new_slot = draw_new_slot(jax.random.fold_in(streams_of[7], 71), 0)
    block_pairs = plant(jax.random.randint(streams_of[3], (NBLK, WB), 0, SLOTS), jax.random.fold_in(streams_of[3], 1), 0, SLOTS - 1).astype(jnp.int32)
    theta_blocks = centred(streams_of[4], (NBLK, TILE, TILE), 1.0, 6.0, ((0, 64),))
    left_env = centred(streams_of[5], (NBLK, WB, TILE, TILE), (TILE * WB) ** -0.5, 0.1875, ((0, 64), (1, 2)))
    right_env = centred(streams_of[6], (WB, TILE, TILE), TILE ** -0.5, 0.375, ((0, 2),))
    return dict(sector_dims=sector_dims, new_owner=new_owner, new_slot=new_slot, block_pairs=block_pairs, theta_blocks=theta_blocks, left_env=left_env, right_env=right_env)


def reference(sector_dims, new_owner, new_slot, block_pairs, theta_blocks, left_env, right_env):
    total = sector_dims.shape[0]
    row_ids = jnp.arange(TILE, dtype=jnp.int32)
    destination = (new_owner * SLOTS + new_slot).astype(jnp.int32)
    anchor = jnp.zeros((total,), jnp.int32).at[destination].set(jnp.arange(total, dtype=jnp.int32))
    grouped = anchor.reshape(N_SEC, SLOTS)
    pair_groups = block_pairs.reshape(N_SEC, SLOTS, WB)
    channel = jnp.arange(WB, dtype=jnp.int32)[None, :]

    def one_holder(inputs):
        members, partners = inputs
        keep = row_ids[None, :] < sector_dims[members][:, None]
        theta_new = jnp.where(keep[:, :, None], theta_blocks[members], jnp.zeros((), theta_blocks.dtype))
        left_new = jnp.where(keep[:, None, :, None], left_env[members], jnp.zeros((), left_env.dtype))
        transfer = jnp.einsum("prc,wcn->pwrn", theta_new.astype(jnp.float32), right_env.astype(jnp.float32)).astype(jnp.bfloat16)
        partner = transfer[partners, channel]
        return jnp.einsum("swrc,swcn->rsn", left_new.astype(jnp.float32), partner.astype(jnp.float32))

    stacked = lax.map(one_holder, (grouped, pair_groups))
    applied = jnp.transpose(stacked, (1, 0, 2, 3)).reshape(TILE, total, TILE)
    return applied.astype(jnp.bfloat16)
```

```python
import functools

import jax
import jax.numpy as jnp
from jax import lax
from jax.experimental import pallas as pl
from jax.experimental.pallas import tpu as pltpu
from jax.sharding import PartitionSpec as P

SWAP = [(0, 1), (1, 0)]
GROUP = 16


def pack_kernel(owner_ref, core_ref, theta_ref, left_ref, out_ref, sems):
    slots, channels, tile, _ = left_ref.shape
    half, quarter = tile // 2, tile // 4
    core = core_ref[0]

    def send(i, carry):
        owner = owner_ref[i]
        for h in range(2):
            place = 2 * owner + h
            for w in range(channels):
                pltpu.make_async_copy(
                    left_ref.at[i, w, pl.ds(h * half, half)],
                    out_ref.at[place, pl.ds(w * half, half)],
                    sems.at[i],
                ).start()
            first = pl.multiple_of(h * half + core * quarter, quarter)
            pltpu.make_async_copy(
                theta_ref.at[i, pl.ds(first, quarter)],
                out_ref.at[place, pl.ds(channels * half, quarter)],
                sems.at[i],
            ).start()
        return carry

    lax.fori_loop(0, slots, send, 0)

    def settle(i, carry):
        pair = out_ref.at[pl.ds(2 * owner_ref[i], 2)]
        pltpu.make_async_copy(pair, pair, sems.at[i]).wait()
        return carry

    lax.fori_loop(0, slots, settle, 0)


def pack(new_owner, core, theta_blocks, left_env, peers):
    slots, channels, tile, cols = left_env.shape
    rows = channels * tile // 2 + tile // 4
    moved = 2 * slots * 2 * rows * cols * 2
    return pl.pallas_call(
        pack_kernel,
        grid_spec=pltpu.PrefetchScalarGridSpec(
            num_scalar_prefetch=2,
            grid=(),
            in_specs=[pl.BlockSpec(memory_space=pltpu.HBM)] * 2,
            out_specs=pl.BlockSpec(memory_space=pltpu.HBM),
            scratch_shapes=[pltpu.SemaphoreType.DMA((slots,))],
        ),
        out_shape=jax.ShapeDtypeStruct((2 * peers, rows, cols), theta_blocks.dtype),
        cost_estimate=pl.CostEstimate(flops=0, bytes_accessed=moved, transcendentals=0),
        name="pack_parcels",
    )(new_owner, core, theta_blocks, left_env)


def apply_kernel(
    anchor_ref, dims_ref, pairs_ref, core_ref,
    got_ref, other_ref, right_ref, out_ref,
    theta, left, transfer, rows_f32, theta_sems, left_sems,
):
    slots, tile, cols = theta.shape
    channels = right_ref.shape[0]
    half, quarter = tile // 2, tile // 4
    core = core_ref[0]
    bulk = got_ref.shape[1] - quarter

    def fetch_theta(j, carry):
        source = anchor_ref[j]
        for c in range(2):
            mine = pl.multiple_of(core * half + c * quarter, quarter)
            theirs = pl.multiple_of((1 - core) * half + c * quarter, quarter)
            pltpu.make_async_copy(
                got_ref.at[2 * source + c, pl.ds(bulk, quarter)],
                theta.at[j, pl.ds(mine, quarter)],
                theta_sems.at[j],
            ).start()
            pltpu.make_async_copy(
                other_ref.at[2 * source + c],
                theta.at[j, pl.ds(theirs, quarter)],
                theta_sems.at[j],
            ).start()
        return carry

    def fetch_left(j, carry):
        source = anchor_ref[j]
        for c in range(2):
            pltpu.make_async_copy(
                got_ref.at[2 * source + c, pl.ds(0, bulk)],
                left.at[j, pl.ds(c * bulk, bulk)],
                left_sems.at[j],
            ).start()
        return carry

    lax.fori_loop(0, slots, fetch_theta, 0)
    lax.fori_loop(0, slots, fetch_left, 0)

    row_ids = lax.broadcasted_iota(jnp.int32, (tile, cols), 0)

    def build(j, carry):
        pltpu.make_async_copy(theta.at[j], theta.at[j], theta_sems.at[j]).wait()
        live = jnp.where(row_ids < dims_ref[j], theta[j].astype(jnp.float32), 0.0)
        live = live.astype(theta.dtype)
        for w in range(channels):
            transfer[j, w] = jnp.dot(
                live, right_ref[w], preferred_element_type=jnp.float32
            ).astype(transfer.dtype)
        return carry

    lax.fori_loop(0, slots, build, 0)

    half_ids = lax.broadcasted_iota(jnp.int32, (half, cols), 0) + core * half

    for g in range(slots // GROUP):

        def contract(k, carry):
            j = g * GROUP + k
            pltpu.make_async_copy(left.at[j], left.at[j], left_sems.at[j]).wait()
            total = jnp.zeros((half, cols), jnp.float32)
            for w in range(channels):
                total += jnp.dot(
                    left[j, w * half:(w + 1) * half],
                    transfer[pairs_ref[w, j], w],
                    preferred_element_type=jnp.float32,
                )
            total = jnp.where(half_ids < dims_ref[j], total, 0.0)
            rows_f32[:, pl.ds(k, half, stride=GROUP)] = jnp.stack(
                [total[:, :128], total[:, 128:]]
            )
            return carry

        lax.fori_loop(0, GROUP, contract, 0)
        for side in range(2):
            out_ref[:, g * GROUP:(g + 1) * GROUP, side * 128:(side + 1) * 128] = (
                rows_f32[side].reshape(half, GROUP, 128).astype(out_ref.dtype)
            )


def apply(anchor, dims, pairs, core, got, other, right, dtype):
    channels, tile, cols = right.shape
    slots = anchor.shape[0]
    half = tile // 2
    flops = 2 * slots * channels * (tile + half) * tile * cols
    moved = 2 * slots * cols * (tile + channels * half + half)
    return pl.pallas_call(
        apply_kernel,
        grid_spec=pltpu.PrefetchScalarGridSpec(
            num_scalar_prefetch=4,
            grid=(),
            in_specs=[
                pl.BlockSpec(memory_space=pltpu.HBM),
                pl.BlockSpec(memory_space=pltpu.HBM),
                pl.BlockSpec(memory_space=pltpu.VMEM),
            ],
            out_specs=pl.BlockSpec(memory_space=pltpu.VMEM),
            scratch_shapes=[
                pltpu.VMEM((slots, tile, cols), dtype),
                pltpu.VMEM((slots, channels * half, cols), dtype),
                pltpu.VMEM((slots, channels, tile, cols), dtype),
                pltpu.VMEM((2, half * GROUP, 128), jnp.float32),
                pltpu.SemaphoreType.DMA((slots,)),
                pltpu.SemaphoreType.DMA((slots,)),
            ],
        ),
        out_shape=jax.ShapeDtypeStruct((half, slots, cols), dtype),
        compiler_params=pltpu.CompilerParams(vmem_limit_bytes=58 << 20),
        cost_estimate=pl.CostEstimate(flops=flops, bytes_accessed=moved, transcendentals=0),
        name="transfer_and_apply",
    )(anchor, dims, pairs, core, got, other, right)


def on_device(sector_dims, new_owner, new_slot, block_pairs, theta_blocks, left_env, right_env):
    peers = lax.axis_size("sec")
    slots, channels, tile, _ = left_env.shape
    me = lax.axis_index("sec")
    core = lax.axis_index("mpo")
    core_word = core.astype(jnp.int32).reshape(1)

    tables = jnp.concatenate(
        [new_owner[None], new_slot[None], sector_dims[None], block_pairs.T], axis=0
    )
    tables = lax.all_gather(tables, ("sec", "mpo"), axis=0, tiled=False)
    right_other = lax.ppermute(right_env, "mpo", SWAP)

    parcels = pack(new_owner, core_word, theta_blocks, left_env, peers)
    got = lax.all_to_all(parcels, ("sec", "mpo"), split_axis=0, concat_axis=0, tiled=True)
    got, tables, right_other = lax.optimization_barrier((got, tables, right_other))
    bulk = channels * tile // 2
    other = lax.ppermute(got[:, bulk:], "mpo", SWAP)

    tables = tables.reshape(peers, 2, 3 + channels, slots)
    owner, slot, live = tables[:, 0, 0], tables[:, 0, 1], tables[:, 0, 2]
    lands = (owner == me)[:, :, None] & (
        slot[:, :, None] == jnp.arange(slots, dtype=jnp.int32)[None, None, :]
    )
    source = jnp.arange(peers, dtype=jnp.int32)[:, None, None]
    anchor = jnp.sum(jnp.where(lands, source, 0), axis=(0, 1))
    dims = jnp.sum(jnp.where(lands, live[:, :, None], 0), axis=(0, 1))
    pairs = lax.dynamic_index_in_dim(tables, me, 0, keepdims=False)[:, 3:].reshape(
        2 * channels, slots
    )
    first_right = jnp.where(core == 0, right_env, right_other)
    second_right = jnp.where(core == 0, right_other, right_env)
    right = jnp.concatenate([first_right, second_right], axis=0)
    return apply(anchor, dims, pairs, core_word, got, other, right, theta_blocks.dtype)


def solution(mesh):
    return jax.shard_map(
        on_device,
        mesh=mesh,
        in_specs=(
            P("sec"),
            P("sec"),
            P("sec"),
            P("sec", "mpo"),
            P("sec", None, None),
            P("sec", "mpo", None, None),
            P("mpo", None, None),
        ),
        out_specs=P("mpo", "sec", None),
        check_vma=False,
    )
```

```python
import functools

import jax
import jax.numpy as jnp
from jax import lax
from jax.experimental import pallas as pl
from jax.experimental.pallas import tpu as pltpu
from jax.sharding import PartitionSpec as P

SWAP = [(0, 1), (1, 0)]
GROUP = 16
TAIL = 8


def pack_kernel(
    owner_ref, slot_ref, dims_ref, core_ref, theta_ref, left_ref, out_ref,
    staged, blank, load_sems, store_sems, blank_sem,
):
    slots, channels, tile, cols = left_ref.shape
    half, quarter = tile // 2, tile // 4
    bulk = channels * half
    core = core_ref[0]

    def load(i, carry):
        for h in range(2):
            for w in range(channels):
                pltpu.make_async_copy(
                    left_ref.at[i, w, pl.ds(h * half, half)],
                    staged.at[i, h, pl.ds(w * half, half)],
                    load_sems.at[i],
                ).start()
            first = pl.multiple_of(h * half + core * quarter, quarter)
            pltpu.make_async_copy(
                theta_ref.at[i, pl.ds(first, quarter)],
                staged.at[i, h, pl.ds(bulk, quarter)],
                load_sems.at[i],
            ).start()
        return carry

    lax.fori_loop(0, slots, load, 0)

    blank[...] = jnp.zeros_like(blank)
    clear = pltpu.make_async_copy(
        blank, out_ref.at[:, pl.ds(bulk + quarter, TAIL)], blank_sem
    )
    clear.start()
    clear.wait()
    tail_rows = lax.broadcasted_iota(jnp.int32, (TAIL, cols), 0)

    def store(i, carry):
        note = jnp.where(tail_rows == 0, slot_ref[i] + 1, dims_ref[i])
        note = note.astype(jnp.float32).astype(staged.dtype)
        for h in range(2):
            staged[i, h, bulk + quarter:] = note
        body = staged.at[i, :, pl.ds(0, bulk + quarter)]
        pltpu.make_async_copy(body, body, load_sems.at[i]).wait()
        place = 2 * owner_ref[i]
        pltpu.make_async_copy(
            staged.at[i], out_ref.at[pl.ds(place, 2)], store_sems.at[i]
        ).start()
        return carry

    lax.fori_loop(0, slots, store, 0)

    def settle(i, carry):
        place = 2 * owner_ref[i]
        pltpu.make_async_copy(
            staged.at[i], out_ref.at[pl.ds(place, 2)], store_sems.at[i]
        ).wait()
        return carry

    lax.fori_loop(0, slots, settle, 0)


def pack(new_owner, new_slot, sector_dims, core, theta_blocks, left_env, peers):
    slots, channels, tile, cols = left_env.shape
    rows = channels * tile // 2 + tile // 4 + TAIL
    dtype = theta_blocks.dtype
    moved = 2 * slots * 2 * rows * cols * 2
    return pl.pallas_call(
        pack_kernel,
        grid_spec=pltpu.PrefetchScalarGridSpec(
            num_scalar_prefetch=4,
            grid=(),
            in_specs=[pl.BlockSpec(memory_space=pltpu.HBM)] * 2,
            out_specs=pl.BlockSpec(memory_space=pltpu.HBM),
            scratch_shapes=[
                pltpu.VMEM((slots, 2, rows, cols), dtype),
                pltpu.VMEM((2 * peers, TAIL, cols), dtype),
                pltpu.SemaphoreType.DMA((slots,)),
                pltpu.SemaphoreType.DMA((slots,)),
                pltpu.SemaphoreType.DMA,
            ],
        ),
        out_shape=jax.ShapeDtypeStruct((2 * peers, rows, cols), dtype),
        compiler_params=pltpu.CompilerParams(vmem_limit_bytes=40 << 20),
        cost_estimate=pl.CostEstimate(flops=0, bytes_accessed=moved, transcendentals=0),
        name="pack_parcels",
    )(new_owner, new_slot, sector_dims, core, theta_blocks, left_env)


def apply_kernel(
    anchor_ref, dims_ref, pairs_ref, core_ref,
    got_ref, other_ref, right_ref, out_ref,
    theta, left, transfer, rows_f32, theta_sems, left_sems,
):
    slots, tile, cols = theta.shape
    channels = right_ref.shape[0]
    half, quarter = tile // 2, tile // 4
    core = core_ref[0]
    bulk = got_ref.shape[1] - quarter - TAIL

    def fetch_theta(j, carry):
        source = anchor_ref[j]
        for c in range(2):
            mine = pl.multiple_of(core * half + c * quarter, quarter)
            theirs = pl.multiple_of((1 - core) * half + c * quarter, quarter)
            pltpu.make_async_copy(
                got_ref.at[2 * source + c, pl.ds(bulk, quarter)],
                theta.at[j, pl.ds(mine, quarter)],
                theta_sems.at[j],
            ).start()
            pltpu.make_async_copy(
                other_ref.at[2 * source + c],
                theta.at[j, pl.ds(theirs, quarter)],
                theta_sems.at[j],
            ).start()
        return carry

    def fetch_left(j, carry):
        source = anchor_ref[j]
        for c in range(2):
            pltpu.make_async_copy(
                got_ref.at[2 * source + c, pl.ds(0, bulk)],
                left.at[j, pl.ds(c * bulk, bulk)],
                left_sems.at[j],
            ).start()
        return carry

    lax.fori_loop(0, slots, fetch_theta, 0)
    lax.fori_loop(0, slots, fetch_left, 0)

    row_ids = lax.broadcasted_iota(jnp.int32, (tile, cols), 0)

    def build(j, carry):
        pltpu.make_async_copy(theta.at[j], theta.at[j], theta_sems.at[j]).wait()
        live = jnp.where(row_ids < dims_ref[j], theta[j].astype(jnp.float32), 0.0)
        live = live.astype(theta.dtype)
        for w in range(channels):
            transfer[j, w] = jnp.dot(
                live, right_ref[w], preferred_element_type=jnp.float32
            ).astype(transfer.dtype)
        return carry

    lax.fori_loop(0, slots, build, 0)

    half_ids = lax.broadcasted_iota(jnp.int32, (half, cols), 0) + core * half

    for g in range(slots // GROUP):

        def contract(k, carry):
            j = g * GROUP + k
            pltpu.make_async_copy(left.at[j], left.at[j], left_sems.at[j]).wait()
            total = jnp.zeros((half, cols), jnp.float32)
            for w in range(channels):
                total += jnp.dot(
                    left[j, w * half:(w + 1) * half],
                    transfer[pairs_ref[w, j], w],
                    preferred_element_type=jnp.float32,
                )
            total = jnp.where(half_ids < dims_ref[j], total, 0.0)
            rows_f32[:, pl.ds(k, half, stride=GROUP)] = jnp.stack(
                [total[:, :128], total[:, 128:]]
            )
            return carry

        lax.fori_loop(0, GROUP, contract, 0)
        for side in range(2):
            out_ref[:, g * GROUP:(g + 1) * GROUP, side * 128:(side + 1) * 128] = (
                rows_f32[side].reshape(half, GROUP, 128).astype(out_ref.dtype)
            )


def apply(anchor, dims, pairs, core, got, other, right, dtype):
    channels, tile, cols = right.shape
    slots = anchor.shape[0]
    half = tile // 2
    flops = 2 * slots * channels * (tile + half) * tile * cols
    moved = 2 * slots * cols * (tile + channels * half + half)
    return pl.pallas_call(
        apply_kernel,
        grid_spec=pltpu.PrefetchScalarGridSpec(
            num_scalar_prefetch=4,
            grid=(),
            in_specs=[
                pl.BlockSpec(memory_space=pltpu.HBM),
                pl.BlockSpec(memory_space=pltpu.HBM),
                pl.BlockSpec(memory_space=pltpu.VMEM),
            ],
            out_specs=pl.BlockSpec(memory_space=pltpu.VMEM),
            scratch_shapes=[
                pltpu.VMEM((slots, tile, cols), dtype),
                pltpu.VMEM((slots, channels * half, cols), dtype),
                pltpu.VMEM((slots, channels, tile, cols), dtype),
                pltpu.VMEM((2, half * GROUP, 128), jnp.float32),
                pltpu.SemaphoreType.DMA((slots,)),
                pltpu.SemaphoreType.DMA((slots,)),
            ],
        ),
        out_shape=jax.ShapeDtypeStruct((half, slots, cols), dtype),
        compiler_params=pltpu.CompilerParams(vmem_limit_bytes=58 << 20),
        cost_estimate=pl.CostEstimate(flops=flops, bytes_accessed=moved, transcendentals=0),
        name="transfer_and_apply",
    )(anchor, dims, pairs, core, got, other, right)


def on_device(sector_dims, new_owner, new_slot, block_pairs, theta_blocks, left_env, right_env):
    peers = lax.axis_size("sec")
    slots, channels, tile, _ = left_env.shape
    core = lax.axis_index("mpo")
    core_word = core.astype(jnp.int32).reshape(1)

    right_other = lax.ppermute(right_env, "mpo", SWAP)
    pairs_other = lax.ppermute(block_pairs, "mpo", SWAP)
    parcels = pack(
        new_owner, new_slot, sector_dims, core_word, theta_blocks, left_env, peers
    )
    parcels, right_other, pairs_other = lax.optimization_barrier(
        (parcels, right_other, pairs_other)
    )
    got = lax.all_to_all(parcels, ("sec", "mpo"), split_axis=0, concat_axis=0, tiled=True)
    got, right_other, pairs_other, core = lax.optimization_barrier(
        (got, right_other, pairs_other, core)
    )
    bulk = channels * tile // 2
    notes = bulk + tile // 4
    other = lax.ppermute(got[:, bulk:notes], "mpo", SWAP)

    slot = got[0::2, notes, 0].astype(jnp.int32)
    live = got[0::2, notes + 1, 0].astype(jnp.int32)
    lands = slot[None, :] == jnp.arange(1, slots + 1, dtype=jnp.int32)[:, None]
    source = jnp.arange(peers, dtype=jnp.int32)[None, :]
    anchor = jnp.sum(jnp.where(lands, source, 0), axis=1)
    dims = jnp.sum(jnp.where(lands, live[None, :], 0), axis=1)
    first = core == 0
    pairs = jnp.concatenate(
        [jnp.where(first, block_pairs, pairs_other), jnp.where(first, pairs_other, block_pairs)],
        axis=1,
    ).T
    right = jnp.concatenate(
        [jnp.where(first, right_env, right_other), jnp.where(first, right_other, right_env)],
        axis=0,
    )
    return apply(anchor, dims, pairs, core_word, got, other, right, theta_blocks.dtype)


def solution(mesh):
    return jax.shard_map(
        on_device,
        mesh=mesh,
        in_specs=(
            P("sec"),
            P("sec"),
            P("sec"),
            P("sec", "mpo"),
            P("sec", None, None),
            P("sec", "mpo", None, None),
            P("mpo", None, None),
        ),
        out_specs=P("mpo", "sec", None),
        check_vma=False,
    )
```

```python
import jax
import jax.numpy as jnp
from jax import lax
from jax.experimental import pallas as pl
from jax.experimental.pallas import tpu as pltpu
from jax.sharding import PartitionSpec as P

SWAP = [(0, 1), (1, 0)]
TAIL = 8
GROUP = 16
STEP = 4
LANES = 128
HBM = pl.BlockSpec(memory_space=pltpu.HBM)


def copy(source, target, sem):
    return pltpu.make_async_copy(source, target, sem)


def pack_kernel(
    owner_ref, slot_ref, dims_ref, core_ref, theta_ref, left_ref, out_ref,
    staged, blank, load_sems, store_sems, blank_sem,
):
    slots, channels, _, half, cols = left_ref.shape
    quarter = half // 2
    bulk = channels * half
    core = core_ref[0]

    def load(i, carry):
        for h in range(2):
            copy(
                left_ref.at[i, :, h],
                staged.at[i, h, pl.ds(0, bulk)].reshape(channels, half, cols),
                load_sems.at[i],
            ).start()
        copy(
            theta_ref.at[i, :, core],
            staged.at[i, :, pl.ds(bulk, quarter)],
            load_sems.at[i],
        ).start()
        return carry

    lax.fori_loop(0, slots, load, 0)

    blank[...] = jnp.zeros_like(blank)
    clear = copy(blank, out_ref.at[:, pl.ds(bulk + quarter, TAIL)], blank_sem)
    clear.start()
    clear.wait()
    tail_rows = lax.broadcasted_iota(jnp.int32, (TAIL, cols), 0)

    def store(i, carry):
        note = jnp.where(tail_rows == 0, slot_ref[i] + 1, dims_ref[i])
        note = note.astype(jnp.float32).astype(staged.dtype)
        for h in range(2):
            staged[i, h, bulk + quarter:] = note
        body = staged.at[i, :, pl.ds(0, bulk + quarter)]
        copy(body, body, load_sems.at[i]).wait()
        place = 2 * owner_ref[i]
        copy(staged.at[i], out_ref.at[pl.ds(place, 2)], store_sems.at[i]).start()
        return carry

    lax.fori_loop(0, slots, store, 0)

    def settle(i, carry):
        place = 2 * owner_ref[i]
        copy(staged.at[i], out_ref.at[pl.ds(place, 2)], store_sems.at[i]).wait()
        return carry

    lax.fori_loop(0, slots, settle, 0)


def pack(new_owner, new_slot, sector_dims, core, theta_blocks, left_env, peers):
    slots, channels, tile, cols = left_env.shape
    half, quarter = tile // 2, tile // 4
    rows = channels * half + quarter + TAIL
    dtype = theta_blocks.dtype
    moved = 2 * slots * 2 * rows * cols * 2
    return pl.pallas_call(
        pack_kernel,
        grid_spec=pltpu.PrefetchScalarGridSpec(
            num_scalar_prefetch=4,
            grid=(),
            in_specs=[HBM] * 2,
            out_specs=HBM,
            scratch_shapes=[
                pltpu.VMEM((slots, 2, rows, cols), dtype),
                pltpu.VMEM((2 * peers, TAIL, cols), dtype),
                pltpu.SemaphoreType.DMA((slots,)),
                pltpu.SemaphoreType.DMA((slots,)),
                pltpu.SemaphoreType.DMA,
            ],
        ),
        out_shape=jax.ShapeDtypeStruct((2 * peers, rows, cols), dtype),
        compiler_params=pltpu.CompilerParams(vmem_limit_bytes=60 << 20),
        cost_estimate=pl.CostEstimate(flops=0, bytes_accessed=moved, transcendentals=0),
        name="pack_parcels",
    )(
        new_owner, new_slot, sector_dims, core,
        theta_blocks.reshape(slots, 2, 2, quarter, cols),
        left_env.reshape(slots, channels, 2, half, cols),
    )


def split_kernel(got_ref, quarters_ref, places_ref, notes, quarter_sem, note_sem):
    parcels, quarter, _ = quarters_ref.shape
    end = got_ref.shape[1]
    theta = copy(
        got_ref.at[:, pl.ds(end - TAIL - quarter, quarter)], quarters_ref, quarter_sem
    )
    tails = copy(
        got_ref.at[:, pl.ds(end - TAIL, TAIL), pl.ds(0, LANES)], notes, note_sem
    )
    tails.start()
    theta.start()
    tails.wait()
    tail = notes[...].astype(jnp.float32)
    row = lax.broadcasted_iota(jnp.int32, tail.shape, 1)
    slot = jnp.sum(jnp.where(row == 0, tail, 0.0), axis=1)
    live = jnp.sum(jnp.where(row == 1, tail, 0.0), axis=1)
    parcel = lax.broadcasted_iota(jnp.int32, slot.shape, 0)
    wanted = lax.broadcasted_iota(jnp.int32, slot.shape, 1) + 1
    lands = (slot.astype(jnp.int32) == wanted) & (parcel % 2 == 0)
    anchor = jnp.sum(jnp.where(lands, parcel, 0), axis=0, keepdims=True)
    dims = jnp.sum(jnp.where(lands, live.astype(jnp.int32), 0), axis=0, keepdims=True)
    places_ref[0:1, :] = anchor
    places_ref[1:2, :] = dims
    theta.wait()


def split(got, quarter):
    parcels, rows, cols = got.shape
    return pl.pallas_call(
        split_kernel,
        in_specs=[HBM],
        out_specs=[pl.BlockSpec(memory_space=pltpu.VMEM)] * 2,
        scratch_shapes=[
            pltpu.VMEM((parcels, TAIL, LANES), got.dtype),
            pltpu.SemaphoreType.DMA,
            pltpu.SemaphoreType.DMA,
        ],
        out_shape=[
            jax.ShapeDtypeStruct((parcels, quarter, cols), got.dtype),
            jax.ShapeDtypeStruct((2, LANES), jnp.int32),
        ],
        compiler_params=pltpu.CompilerParams(vmem_limit_bytes=60 << 20),
        name="split_parcels",
    )(got)


def apply_kernel(
    places_ref, pairs_ref, core_ref, got_ref, other_ref, right_ref, out_ref,
    theta, left, inner, rows_f32, theta_sems, left_sems,
):
    slots, _, _, quarter, cols = theta.shape
    channels = left.shape[1] * left.shape[2]
    half, tile = 2 * quarter, 4 * quarter
    bulk = channels * half // 2
    core = core_ref[0]

    def fetch_theta(j, carry):
        source = places_ref[0, j]
        copy(
            got_ref.at[pl.ds(source, 2), pl.ds(bulk, quarter)],
            theta.at[j, core],
            theta_sems.at[j],
        ).start()
        copy(other_ref.at[pl.ds(source, 2)], theta.at[j, 1 - core], theta_sems.at[j]).start()
        return carry

    def fetch_left(j, carry):
        source = places_ref[0, j]
        copy(
            got_ref.at[pl.ds(source, 2), pl.ds(0, bulk)],
            left.at[j].reshape(2, bulk, cols),
            left_sems.at[j],
        ).start()
        return carry

    lax.fori_loop(0, slots, fetch_theta, 0)
    lax.fori_loop(0, slots, fetch_left, 0)

    strip = 16
    strip_rows = lax.broadcasted_iota(jnp.int32, (strip, cols), 0)

    def trim(j, carry):
        copy(theta.at[j], theta.at[j], theta_sems.at[j]).wait()
        live = places_ref[1, j]
        block = theta.at[j].reshape(tile, cols)

        def clear(t, inner_carry):
            first = pl.multiple_of(t * strip, strip)
            rows = block[pl.ds(first, strip)].astype(jnp.float32)
            rows = jnp.where(strip_rows + first < live, rows, 0.0)
            block[pl.ds(first, strip)] = rows.astype(theta.dtype)
            return inner_carry

        return lax.fori_loop(live // strip, tile // strip, clear, carry)

    lax.fori_loop(0, slots, trim, 0)

    half_ids = lax.broadcasted_iota(jnp.int32, (half, cols), 0) + core * half

    for g in range(slots // GROUP):

        def contract(b, carry):
            for k in range(STEP):
                j = g * GROUP + b * STEP + k
                copy(left.at[j], left.at[j], left_sems.at[j]).wait()
                for w in range(channels):
                    partner = theta[pairs_ref[w, j]].reshape(tile, cols)
                    inner[k * half:(k + 1) * half, w * cols:(w + 1) * cols] = jnp.dot(
                        left[j, w // 2, w % 2],
                        partner,
                        preferred_element_type=jnp.float32,
                    ).astype(inner.dtype)
            total = jnp.dot(
                inner[...], right_ref[...], preferred_element_type=jnp.float32
            )
            for k in range(STEP):
                j = g * GROUP + b * STEP + k
                kept = jnp.where(
                    half_ids < places_ref[1, j], total[k * half:(k + 1) * half], 0.0
                )
                for side in range(2):
                    rows_f32[side, pl.ds(b * STEP + k, half, stride=GROUP)] = kept[
                        :, side * LANES:(side + 1) * LANES
                    ]
            return carry

        lax.fori_loop(0, GROUP // STEP, contract, 0)
        for side in range(2):
            out_ref[:, g * GROUP:(g + 1) * GROUP, side * LANES:(side + 1) * LANES] = (
                rows_f32[side].reshape(half, GROUP, LANES).astype(out_ref.dtype)
            )


def apply(places, pairs, core, got, other, right, dtype):
    channels, tile, cols = right.shape
    slots = pairs.shape[1]
    half, quarter = tile // 2, tile // 4
    flops = 4 * slots * channels * half * tile * cols
    moved = 2 * slots * cols * (tile + channels * half + half)
    return pl.pallas_call(
        apply_kernel,
        grid_spec=pltpu.PrefetchScalarGridSpec(
            num_scalar_prefetch=3,
            grid=(),
            in_specs=[HBM, HBM, pl.BlockSpec(memory_space=pltpu.VMEM)],
            out_specs=pl.BlockSpec(memory_space=pltpu.VMEM),
            scratch_shapes=[
                pltpu.VMEM((slots, 2, 2, quarter, cols), dtype),
                pltpu.VMEM((slots, 2, channels // 2, half, cols), dtype),
                pltpu.VMEM((STEP * half, channels * cols), dtype),
                pltpu.VMEM((2, half * GROUP, LANES), jnp.float32),
                pltpu.SemaphoreType.DMA((slots,)),
                pltpu.SemaphoreType.DMA((slots,)),
            ],
        ),
        out_shape=jax.ShapeDtypeStruct((half, slots, cols), dtype),
        compiler_params=pltpu.CompilerParams(vmem_limit_bytes=60 << 20),
        cost_estimate=pl.CostEstimate(flops=flops, bytes_accessed=moved, transcendentals=0),
        name="contract",
    )(places, pairs, core, got, other, right.reshape(channels * tile, cols))


def on_device(sector_dims, new_owner, new_slot, block_pairs, theta_blocks, left_env, right_env):
    peers = lax.axis_size("sec")
    core = lax.axis_index("mpo")
    core_word = core.astype(jnp.int32).reshape(1)

    right_other = lax.ppermute(right_env, "mpo", SWAP)
    pairs_other = lax.ppermute(block_pairs, "mpo", SWAP)
    parcels = pack(
        new_owner, new_slot, sector_dims, core_word, theta_blocks, left_env, peers
    )
    parcels, right_other, pairs_other = lax.optimization_barrier(
        (parcels, right_other, pairs_other)
    )
    got = lax.all_to_all(parcels, ("sec", "mpo"), split_axis=0, concat_axis=0, tiled=True)
    got, right_other, pairs_other, core = lax.optimization_barrier(
        (got, right_other, pairs_other, core)
    )
    quarters, places = split(got, theta_blocks.shape[1] // 4)
    other = lax.ppermute(quarters, "mpo", SWAP)
    first = core == 0
    pairs = jnp.concatenate(
        [jnp.where(first, block_pairs, pairs_other), jnp.where(first, pairs_other, block_pairs)],
        axis=1,
    ).T
    right = jnp.concatenate(
        [jnp.where(first, right_env, right_other), jnp.where(first, right_other, right_env)],
        axis=0,
    )
    return apply(places, pairs, core_word, got, other, right, theta_blocks.dtype)


def solution(mesh):
    return jax.shard_map(
        on_device,
        mesh=mesh,
        in_specs=(
            P("sec"),
            P("sec"),
            P("sec"),
            P("sec", "mpo"),
            P("sec", None, None),
            P("sec", "mpo", None, None),
            P("mpo", None, None),
        ),
        out_specs=P("mpo", "sec", None),
        check_vma=False,
    )
```

```python
import jax
import jax.numpy as jnp
from jax import lax
from jax.experimental import pallas as pl
from jax.experimental.pallas import tpu as pltpu
from jax.sharding import PartitionSpec as P

SWAP = [(0, 1), (1, 0)]
TAIL = 8
GROUP = 16
STEP = 8
LANES = 128
HBM = pl.BlockSpec(memory_space=pltpu.HBM)


def copy(source, target, sem):
    return pltpu.make_async_copy(source, target, sem)


def pack_kernel(
    owner_ref, slot_ref, dims_ref, core_ref, theta_ref, left_ref, out_ref,
    staged, blank, load_sems, store_sems, blank_sem,
):
    slots, channels, _, half, cols = left_ref.shape
    quarter = half // 2
    bulk = channels * half
    core = core_ref[0]

    def load(i, carry):
        for h in range(2):
            copy(
                left_ref.at[i, :, h],
                staged.at[i, h, pl.ds(0, bulk)].reshape(channels, half, cols),
                load_sems.at[i],
            ).start()
        copy(
            theta_ref.at[i, :, core],
            staged.at[i, :, pl.ds(bulk, quarter)],
            load_sems.at[i],
        ).start()
        return carry

    lax.fori_loop(0, slots, load, 0)

    blank[...] = jnp.zeros_like(blank)
    clear = copy(blank, out_ref.at[:, pl.ds(bulk + quarter, TAIL)], blank_sem)
    clear.start()
    clear.wait()
    tail_rows = lax.broadcasted_iota(jnp.int32, (TAIL, cols), 0)

    def store(i, carry):
        note = jnp.where(tail_rows == 0, slot_ref[i] + 1, dims_ref[i])
        note = note.astype(jnp.float32).astype(staged.dtype)
        for h in range(2):
            staged[i, h, bulk + quarter:] = note
        body = staged.at[i, :, pl.ds(0, bulk + quarter)]
        copy(body, body, load_sems.at[i]).wait()
        place = 2 * owner_ref[i]
        copy(staged.at[i], out_ref.at[pl.ds(place, 2)], store_sems.at[i]).start()
        return carry

    lax.fori_loop(0, slots, store, 0)

    def settle(i, carry):
        place = 2 * owner_ref[i]
        copy(staged.at[i], out_ref.at[pl.ds(place, 2)], store_sems.at[i]).wait()
        return carry

    lax.fori_loop(0, slots, settle, 0)


def pack(new_owner, new_slot, sector_dims, core, theta_blocks, left_env, peers):
    slots, channels, tile, cols = left_env.shape
    half, quarter = tile // 2, tile // 4
    rows = channels * half + quarter + TAIL
    dtype = theta_blocks.dtype
    moved = 2 * slots * 2 * rows * cols * 2
    return pl.pallas_call(
        pack_kernel,
        grid_spec=pltpu.PrefetchScalarGridSpec(
            num_scalar_prefetch=4,
            grid=(),
            in_specs=[HBM] * 2,
            out_specs=HBM,
            scratch_shapes=[
                pltpu.VMEM((slots, 2, rows, cols), dtype),
                pltpu.VMEM((2 * peers, TAIL, cols), dtype),
                pltpu.SemaphoreType.DMA((slots,)),
                pltpu.SemaphoreType.DMA((slots,)),
                pltpu.SemaphoreType.DMA,
            ],
        ),
        out_shape=jax.ShapeDtypeStruct((2 * peers, rows, cols), dtype),
        compiler_params=pltpu.CompilerParams(vmem_limit_bytes=60 << 20),
        cost_estimate=pl.CostEstimate(flops=0, bytes_accessed=moved, transcendentals=0),
        name="pack_parcels",
    )(
        new_owner, new_slot, sector_dims, core,
        theta_blocks.reshape(slots, 2, 2, quarter, cols),
        left_env.reshape(slots, channels, 2, half, cols),
    )


def split_kernel(got_ref, out_ref, staged, read_sems, write_sems):
    parcels, quarter, _ = staged.shape
    first = got_ref.shape[1] - TAIL - quarter
    parts = read_sems.shape[0]
    size = parcels // parts
    reads, writes = [], []
    for p in range(parts):
        span = pl.ds(p * size, size)
        reads.append(
            copy(got_ref.at[span, pl.ds(first, quarter)], staged.at[span], read_sems.at[p])
        )
        writes.append(copy(staged.at[span], out_ref.at[span], write_sems.at[p]))
        reads[p].start()
    for p in range(parts):
        reads[p].wait()
        writes[p].start()
    for p in range(parts):
        writes[p].wait()


def split(got, quarter):
    parcels, rows, cols = got.shape
    return pl.pallas_call(
        split_kernel,
        in_specs=[HBM],
        out_specs=HBM,
        scratch_shapes=[
            pltpu.VMEM((parcels, quarter, cols), got.dtype),
            pltpu.SemaphoreType.DMA((8,)),
            pltpu.SemaphoreType.DMA((8,)),
        ],
        out_shape=jax.ShapeDtypeStruct((parcels, quarter, cols), got.dtype),
        compiler_params=pltpu.CompilerParams(vmem_limit_bytes=60 << 20),
        name="theta_quarters",
    )(got)


def places_kernel(got_ref, out_ref, notes, note_sem):
    end = got_ref.shape[1]
    tails = copy(got_ref.at[:, pl.ds(end - TAIL, TAIL), pl.ds(0, LANES)], notes, note_sem)
    tails.start()
    tails.wait()
    tail = notes[...].astype(jnp.float32)
    row = lax.broadcasted_iota(jnp.int32, tail.shape, 1)
    slot = jnp.sum(jnp.where(row == 0, tail, 0.0), axis=1)
    live = jnp.sum(jnp.where(row == 1, tail, 0.0), axis=1)
    parcel = lax.broadcasted_iota(jnp.int32, slot.shape, 0)
    wanted = lax.broadcasted_iota(jnp.int32, slot.shape, 1) + 1
    lands = (slot.astype(jnp.int32) == wanted) & (parcel % 2 == 0)
    anchor = jnp.sum(jnp.where(lands, parcel, 0), axis=0, keepdims=True)
    dims = jnp.sum(jnp.where(lands, live.astype(jnp.int32), 0), axis=0, keepdims=True)
    out_ref[0:1, :] = anchor
    out_ref[1:2, :] = dims


def find_places(got):
    parcels = got.shape[0]
    return pl.pallas_call(
        places_kernel,
        in_specs=[HBM],
        out_specs=pl.BlockSpec(memory_space=pltpu.VMEM),
        scratch_shapes=[
            pltpu.VMEM((parcels, TAIL, LANES), got.dtype),
            pltpu.SemaphoreType.DMA,
        ],
        out_shape=jax.ShapeDtypeStruct((2, LANES), jnp.int32),
        compiler_params=pltpu.CompilerParams(vmem_limit_bytes=60 << 20),
        cost_estimate=pl.CostEstimate(flops=0, bytes_accessed=8 << 20, transcendentals=0),
        name="places",
    )(got)


def apply_kernel(
    places_ref, pairs_ref, core_ref, got_ref, other_ref, right_ref, out_ref,
    theta, left, inner, even, odd, turned, theta_sems, left_sems, out_sems,
):
    slots, _, _, quarter, cols = theta.shape
    channels = left.shape[1] * left.shape[2]
    half, tile = 2 * quarter, 4 * quarter
    bulk = channels * half // 2
    core = core_ref[0]
    groups, steps = slots // GROUP, GROUP // STEP
    part = half // steps

    def fetch(j, carry):
        source = places_ref[0, j]
        copy(
            got_ref.at[pl.ds(source, 2), pl.ds(bulk, quarter)],
            theta.at[j, core],
            theta_sems.at[j],
        ).start()
        copy(other_ref.at[pl.ds(source, 2)], theta.at[j, 1 - core], theta_sems.at[j]).start()
        return carry

    lax.fori_loop(0, slots, fetch, 0)

    strip = 16
    strip_rows = lax.broadcasted_iota(jnp.int32, (strip, cols), 0)

    def trim(j, carry):
        copy(
            got_ref.at[pl.ds(places_ref[0, j], 2), pl.ds(0, bulk)],
            left.at[j].reshape(2, bulk, cols),
            left_sems.at[j],
        ).start()
        copy(theta.at[j], theta.at[j], theta_sems.at[j]).wait()
        live = places_ref[1, j]
        block = theta.at[j].reshape(tile, cols)

        def clear(t, inner_carry):
            first = pl.multiple_of(t * strip, strip)
            rows = block[pl.ds(first, strip)].astype(jnp.float32)
            rows = jnp.where(strip_rows + first < live, rows, 0.0)
            block[pl.ds(first, strip)] = rows.astype(theta.dtype)
            return inner_carry

        return lax.fori_loop(live // strip, tile // strip, clear, carry)

    lax.fori_loop(0, slots, trim, 0)

    half_ids = lax.broadcasted_iota(jnp.int32, (half, cols), 0) + core * half

    def turn(g, b):
        first = pl.multiple_of(b * part, part)
        rows = (even, odd)[g % 2][:, pl.ds(first, part), :]
        turned[g, pl.ds(first, part)] = pltpu.einshape("krn->rkn", rows).astype(turned.dtype)

    def write(g):
        return copy(turned.at[g], out_ref.at[:, pl.ds(g * GROUP, GROUP)], out_sems.at[g])

    for g in range(groups):

        def contract(b, carry):
            for k in range(STEP):
                j = g * GROUP + b * STEP + k
                copy(left.at[j], left.at[j], left_sems.at[j]).wait()
            for k in range(STEP):
                j = g * GROUP + b * STEP + k
                for w in range(channels):
                    partner = theta[pairs_ref[w, j]].reshape(tile, cols)
                    inner[k * half:(k + 1) * half, w * cols:(w + 1) * cols] = jnp.dot(
                        left[j, w // 2, w % 2],
                        partner,
                        preferred_element_type=jnp.float32,
                    ).astype(inner.dtype)
            if g > 0:
                turn(g - 1, b)
            total = jnp.dot(
                inner[...], right_ref[...], preferred_element_type=jnp.float32
            )
            for k in range(STEP):
                live = places_ref[1, g * GROUP + b * STEP + k]
                (even, odd)[g % 2][b * STEP + k] = jnp.where(
                    half_ids < live, total[k * half:(k + 1) * half], 0.0
                )
            return carry

        lax.fori_loop(0, steps, contract, 0)
        if g > 0:
            write(g - 1).start()

    for b in range(steps):
        turn(groups - 1, b)
    write(groups - 1).start()
    for g in range(groups):
        write(g).wait()


def apply(places, pairs, core, got, other, right, dtype):
    channels, tile, cols = right.shape
    slots = pairs.shape[1]
    half, quarter = tile // 2, tile // 4
    flops = 4 * slots * channels * half * tile * cols
    moved = 2 * slots * cols * (tile + channels * half + half)
    return pl.pallas_call(
        apply_kernel,
        grid_spec=pltpu.PrefetchScalarGridSpec(
            num_scalar_prefetch=3,
            grid=(),
            in_specs=[HBM, HBM, pl.BlockSpec(memory_space=pltpu.VMEM)],
            out_specs=HBM,
            scratch_shapes=[
                pltpu.VMEM((slots, 2, 2, quarter, cols), dtype),
                pltpu.VMEM((slots, 2, channels // 2, half, cols), dtype),
                pltpu.VMEM((STEP * half, channels * cols), dtype),
                pltpu.VMEM((GROUP, half, cols), jnp.float32),
                pltpu.VMEM((GROUP, half, cols), jnp.float32),
                pltpu.VMEM((slots // GROUP, half, GROUP, cols), dtype),
                pltpu.SemaphoreType.DMA((slots,)),
                pltpu.SemaphoreType.DMA((slots,)),
                pltpu.SemaphoreType.DMA((slots // GROUP,)),
            ],
        ),
        out_shape=jax.ShapeDtypeStruct((half, slots, cols), dtype),
        compiler_params=pltpu.CompilerParams(vmem_limit_bytes=60 << 20),
        cost_estimate=pl.CostEstimate(flops=flops, bytes_accessed=moved, transcendentals=0),
        name="contract",
    )(places, pairs, core, got, other, right.reshape(channels * tile, cols))


def on_device(sector_dims, new_owner, new_slot, block_pairs, theta_blocks, left_env, right_env):
    peers = lax.axis_size("sec")
    core = lax.axis_index("mpo")
    core_word = core.astype(jnp.int32).reshape(1)

    right_other = lax.ppermute(right_env, "mpo", SWAP)
    pairs_other = lax.ppermute(block_pairs, "mpo", SWAP)
    parcels = pack(
        new_owner, new_slot, sector_dims, core_word, theta_blocks, left_env, peers
    )
    parcels, right_other, pairs_other = lax.optimization_barrier(
        (parcels, right_other, pairs_other)
    )
    got = lax.all_to_all(parcels, ("sec", "mpo"), split_axis=0, concat_axis=0, tiled=True)
    got, right_other, pairs_other, core = lax.optimization_barrier(
        (got, right_other, pairs_other, core)
    )
    other = lax.ppermute(split(got, theta_blocks.shape[1] // 4), "mpo", SWAP)
    places = find_places(got)
    first = core == 0
    pairs = jnp.concatenate(
        [jnp.where(first, block_pairs, pairs_other), jnp.where(first, pairs_other, block_pairs)],
        axis=1,
    ).T
    right = jnp.concatenate(
        [jnp.where(first, right_env, right_other), jnp.where(first, right_other, right_env)],
        axis=0,
    )
    return apply(places, pairs, core_word, got, other, right, theta_blocks.dtype)


def solution(mesh):
    return jax.shard_map(
        on_device,
        mesh=mesh,
        in_specs=(
            P("sec"),
            P("sec"),
            P("sec"),
            P("sec", "mpo"),
            P("sec", None, None),
            P("sec", "mpo", None, None),
            P("mpo", None, None),
        ),
        out_specs=P("mpo", "sec", None),
        check_vma=False,
    )
```

```python
import functools

import jax
import jax.numpy as jnp
from jax import lax
from jax.experimental import pallas as pl
from jax.experimental.pallas import tpu as pltpu
from jax.sharding import PartitionSpec as P

SWAP = [(0, 1), (1, 0)]
TAIL = 8
GROUP = 16
STEP = 8
LANES = 128
HBM = pl.BlockSpec(memory_space=pltpu.HBM)


def copy(source, target, sem):
    return pltpu.make_async_copy(source, target, sem)


def pack_kernel(
    owner_ref, slot_ref, dims_ref, core_ref, theta_ref, left_ref, out_ref,
    left, theta, notes, blank, load_sems, store_sems, blank_sem,
):
    slots, channels, _, half, cols = left_ref.shape
    quarter = half // 2
    bulk = channels * half
    sides = cols // LANES
    body = sides * (bulk + quarter)
    core = core_ref[0]

    def load(i, carry):
        copy(left_ref.at[i], left.at[i], load_sems.at[0, i]).start()
        copy(theta_ref.at[i, :, core], theta.at[i], load_sems.at[1, i]).start()
        return carry

    lax.fori_loop(0, slots, load, 0)

    blank[...] = jnp.zeros_like(blank)
    clear = copy(blank, out_ref.at[:, pl.ds(body, TAIL)], blank_sem)
    clear.start()
    clear.wait()
    tail_rows = lax.broadcasted_iota(jnp.int32, (2, TAIL, LANES), 1)

    def store(i, carry):
        text = jnp.where(tail_rows == 0, slot_ref[i] + 1, dims_ref[i])
        notes[i] = text.astype(jnp.float32).astype(notes.dtype)
        place = 2 * owner_ref[i]
        pair = pl.ds(place, 2)
        copy(notes.at[i], out_ref.at[pair, pl.ds(body, TAIL)], store_sems.at[i]).start()
        copy(left_ref.at[i], left.at[i], load_sems.at[0, i]).wait()
        for c in range(sides):
            lanes = pl.ds(c * LANES, LANES)
            for h in range(2):
                copy(
                    left.at[i, :, h, :, lanes],
                    out_ref.at[place + h, pl.ds(c * bulk, bulk)].reshape(
                        channels, half, LANES
                    ),
                    store_sems.at[i],
                ).start()
        copy(theta_ref.at[i, :, core], theta.at[i], load_sems.at[1, i]).wait()
        for c in range(sides):
            copy(
                theta.at[i, :, :, pl.ds(c * LANES, LANES)],
                out_ref.at[pair, pl.ds(sides * bulk + c * quarter, quarter)],
                store_sems.at[i],
            ).start()
        return carry

    lax.fori_loop(0, slots, store, 0)

    def settle(i, carry):
        pair = out_ref.at[pl.ds(2 * owner_ref[i], 2)]
        copy(pair, pair, store_sems.at[i]).wait()
        return carry

    lax.fori_loop(0, slots, settle, 0)


def pack(new_owner, new_slot, sector_dims, core, theta_blocks, left_env, peers):
    slots, channels, tile, cols = left_env.shape
    half, quarter = tile // 2, tile // 4
    rows = (cols // LANES) * (channels * half + quarter) + TAIL
    dtype = theta_blocks.dtype
    moved = 2 * slots * 2 * rows * LANES * 2
    return pl.pallas_call(
        pack_kernel,
        grid_spec=pltpu.PrefetchScalarGridSpec(
            num_scalar_prefetch=4,
            grid=(),
            in_specs=[HBM] * 2,
            out_specs=HBM,
            scratch_shapes=[
                pltpu.VMEM((slots, channels, 2, half, cols), dtype),
                pltpu.VMEM((slots, 2, quarter, cols), dtype),
                pltpu.VMEM((slots, 2, TAIL, LANES), dtype),
                pltpu.VMEM((2 * peers, TAIL, LANES), dtype),
                pltpu.SemaphoreType.DMA((2, slots)),
                pltpu.SemaphoreType.DMA((slots,)),
                pltpu.SemaphoreType.DMA,
            ],
        ),
        out_shape=jax.ShapeDtypeStruct((2 * peers, rows, LANES), dtype),
        compiler_params=pltpu.CompilerParams(vmem_limit_bytes=60 << 20),
        cost_estimate=pl.CostEstimate(flops=0, bytes_accessed=moved, transcendentals=0),
        name="pack_parcels",
    )(
        new_owner, new_slot, sector_dims, core,
        theta_blocks.reshape(slots, 2, 2, quarter, cols),
        left_env.reshape(slots, channels, 2, half, cols),
    )


def split_kernel(first, got_ref, out_ref, staged, read_sems, write_sems):
    parcels, quarter, _ = staged.shape
    parts = read_sems.shape[0]
    size = parcels // parts
    reads, writes = [], []
    for p in range(parts):
        span = pl.ds(p * size, size)
        reads.append(
            copy(got_ref.at[span, pl.ds(first, quarter)], staged.at[span], read_sems.at[p])
        )
        writes.append(copy(staged.at[span], out_ref.at[span], write_sems.at[p]))
        reads[p].start()
    for p in range(parts):
        reads[p].wait()
        writes[p].start()
    for p in range(parts):
        writes[p].wait()


def split(got, first, quarter):
    parcels = got.shape[0]
    return pl.pallas_call(
        functools.partial(split_kernel, first),
        in_specs=[HBM],
        out_specs=HBM,
        scratch_shapes=[
            pltpu.VMEM((parcels, quarter, LANES), got.dtype),
            pltpu.SemaphoreType.DMA((4,)),
            pltpu.SemaphoreType.DMA((4,)),
        ],
        out_shape=jax.ShapeDtypeStruct((parcels, quarter, LANES), got.dtype),
        compiler_params=pltpu.CompilerParams(vmem_limit_bytes=60 << 20),
        cost_estimate=pl.CostEstimate(flops=0, bytes_accessed=8 << 20, transcendentals=0),
        name="theta_quarters",
    )(got)


def places_kernel(got_ref, out_ref, notes, note_sem):
    tails = copy(got_ref.at[:, pl.ds(got_ref.shape[1] - TAIL, TAIL)], notes, note_sem)
    tails.start()
    tails.wait()
    tail = notes[...].astype(jnp.float32)
    row = lax.broadcasted_iota(jnp.int32, tail.shape, 1)
    slot = jnp.sum(jnp.where(row == 0, tail, 0.0), axis=1)
    live = jnp.sum(jnp.where(row == 1, tail, 0.0), axis=1)
    parcel = lax.broadcasted_iota(jnp.int32, slot.shape, 0)
    wanted = lax.broadcasted_iota(jnp.int32, slot.shape, 1) + 1
    lands = (slot.astype(jnp.int32) == wanted) & (parcel % 2 == 0)
    anchor = jnp.sum(jnp.where(lands, parcel, 0), axis=0, keepdims=True)
    dims = jnp.sum(jnp.where(lands, live.astype(jnp.int32), 0), axis=0, keepdims=True)
    out_ref[0:1, :] = anchor
    out_ref[1:2, :] = dims


def find_places(got):
    parcels = got.shape[0]
    return pl.pallas_call(
        places_kernel,
        in_specs=[HBM],
        out_specs=pl.BlockSpec(memory_space=pltpu.VMEM),
        scratch_shapes=[
            pltpu.VMEM((parcels, TAIL, LANES), got.dtype),
            pltpu.SemaphoreType.DMA,
        ],
        out_shape=jax.ShapeDtypeStruct((2, LANES), jnp.int32),
        compiler_params=pltpu.CompilerParams(vmem_limit_bytes=60 << 20),
        cost_estimate=pl.CostEstimate(flops=0, bytes_accessed=8 << 20, transcendentals=0),
        name="places",
    )(got)


def apply_kernel(sides, places_ref, pairs_ref, core_ref, got_ref, *refs):
    others_ref, right_ref, out_ref = refs[:sides], refs[sides], refs[sides + 1]
    theta, left, inner, even, odd, turned, theta_sems, left_sems, out_sems = refs[sides + 2:]
    slots, _, _, quarter, cols = theta.shape
    half, tile, bulk = 2 * quarter, 4 * quarter, left.shape[2]
    channels = 2 * bulk // half
    core = core_ref[0]
    groups, steps = slots // GROUP, GROUP // STEP
    part = half // steps

    def fetch(j, carry):
        pair = pl.ds(places_ref[0, j], 2)
        for c in range(sides):
            lanes = pl.ds(c * LANES, LANES)
            copy(
                got_ref.at[pair, pl.ds(sides * bulk + c * quarter, quarter)],
                theta.at[j, core, :, :, lanes],
                theta_sems.at[j],
            ).start()
            copy(
                others_ref[c].at[pair], theta.at[j, 1 - core, :, :, lanes], theta_sems.at[j]
            ).start()
        return carry

    lax.fori_loop(0, slots, fetch, 0)

    strip = 16
    strip_rows = lax.broadcasted_iota(jnp.int32, (strip, cols), 0)

    def trim(j, carry):
        for c in range(sides):
            copy(
                got_ref.at[pl.ds(places_ref[0, j], 2), pl.ds(c * bulk, bulk)],
                left.at[j, :, :, pl.ds(c * LANES, LANES)],
                left_sems.at[j],
            ).start()
        copy(theta.at[j], theta.at[j], theta_sems.at[j]).wait()
        live = places_ref[1, j]

        block = theta.at[j].reshape(tile, cols)

        def clear(t, inner_carry):
            first = pl.multiple_of(t * strip, strip)
            rows = block[pl.ds(first, strip)].astype(jnp.float32)
            rows = jnp.where(strip_rows + first < live, rows, 0.0)
            block[pl.ds(first, strip)] = rows.astype(theta.dtype)
            return inner_carry

        return lax.fori_loop(live // strip, tile // strip, clear, carry)

    lax.fori_loop(0, slots, trim, 0)

    half_ids = lax.broadcasted_iota(jnp.int32, (half, cols), 0) + core * half

    def turn(g, b):
        first = pl.multiple_of(b * part, part)
        rows = (even, odd)[g % 2][:, pl.ds(first, part), :]
        turned[g, pl.ds(first, part)] = pltpu.einshape("krn->rkn", rows).astype(turned.dtype)

    def write(g):
        return copy(turned.at[g], out_ref.at[:, pl.ds(g * GROUP, GROUP)], out_sems.at[g])

    for g in range(groups):

        def contract(b, carry):
            for k in range(STEP):
                j = g * GROUP + b * STEP + k
                copy(left.at[j], left.at[j], left_sems.at[j]).wait()
            for k in range(STEP):
                j = g * GROUP + b * STEP + k
                for w in range(channels):
                    inner[k * half:(k + 1) * half, w * cols:(w + 1) * cols] = jnp.dot(
                        left[j, w // 2, pl.ds(w % 2 * half, half)],
                        theta[pairs_ref[w, j]].reshape(tile, cols),
                        preferred_element_type=jnp.float32,
                    ).astype(inner.dtype)
            if g > 0:
                turn(g - 1, b)
            total = jnp.dot(
                inner[...], right_ref[...], preferred_element_type=jnp.float32
            )
            for k in range(STEP):
                live = places_ref[1, g * GROUP + b * STEP + k]
                (even, odd)[g % 2][b * STEP + k] = jnp.where(
                    half_ids < live, total[k * half:(k + 1) * half], 0.0
                )
            return carry

        lax.fori_loop(0, steps, contract, 0)
        if g > 0:
            write(g - 1).start()

    for b in range(steps):
        turn(groups - 1, b)
    write(groups - 1).start()
    for g in range(groups):
        write(g).wait()


def apply(places, pairs, core, got, others, right, dtype):
    channels, tile, cols = right.shape
    slots = pairs.shape[1]
    half, quarter = tile // 2, tile // 4
    flops = 4 * slots * channels * half * tile * cols
    moved = 2 * slots * cols * (tile + channels * half + half)
    return pl.pallas_call(
        functools.partial(apply_kernel, cols // LANES),
        grid_spec=pltpu.PrefetchScalarGridSpec(
            num_scalar_prefetch=3,
            grid=(),
            in_specs=[HBM] * (1 + len(others)) + [pl.BlockSpec(memory_space=pltpu.VMEM)],
            out_specs=HBM,
            scratch_shapes=[
                pltpu.VMEM((slots, 2, 2, quarter, cols), dtype),
                pltpu.VMEM((slots, 2, channels * half // 2, cols), dtype),
                pltpu.VMEM((STEP * half, channels * cols), dtype),
                pltpu.VMEM((GROUP, half, cols), jnp.float32),
                pltpu.VMEM((GROUP, half, cols), jnp.float32),
                pltpu.VMEM((slots // GROUP, half, GROUP, cols), dtype),
                pltpu.SemaphoreType.DMA((slots,)),
                pltpu.SemaphoreType.DMA((slots,)),
                pltpu.SemaphoreType.DMA((slots // GROUP,)),
            ],
        ),
        out_shape=jax.ShapeDtypeStruct((half, slots, cols), dtype),
        compiler_params=pltpu.CompilerParams(vmem_limit_bytes=60 << 20),
        cost_estimate=pl.CostEstimate(flops=flops, bytes_accessed=moved, transcendentals=0),
        name="contract",
    )(places, pairs, core, got, *others, right.reshape(channels * tile, cols))


def on_device(sector_dims, new_owner, new_slot, block_pairs, theta_blocks, left_env, right_env):
    peers = lax.axis_size("sec")
    core = lax.axis_index("mpo")
    core_word = core.astype(jnp.int32).reshape(1)

    right_other = lax.ppermute(right_env, "mpo", SWAP)
    pairs_other = lax.ppermute(block_pairs, "mpo", SWAP)
    parcels = pack(
        new_owner, new_slot, sector_dims, core_word, theta_blocks, left_env, peers
    )
    parcels, right_other, pairs_other = lax.optimization_barrier(
        (parcels, right_other, pairs_other)
    )
    got = lax.all_to_all(parcels, ("sec", "mpo"), split_axis=0, concat_axis=0, tiled=True)
    got, right_other, pairs_other, core = lax.optimization_barrier(
        (got, right_other, pairs_other, core)
    )
    channels, tile, cols = left_env.shape[1:]
    bulk = (cols // LANES) * channels * tile // 2
    others = [
        lax.ppermute(split(got, bulk + c * tile // 4, tile // 4), "mpo", SWAP)
        for c in range(cols // LANES)
    ]
    places = find_places(got)
    first = core == 0
    pairs = jnp.concatenate(
        [jnp.where(first, block_pairs, pairs_other), jnp.where(first, pairs_other, block_pairs)],
        axis=1,
    ).T
    right = jnp.concatenate(
        [jnp.where(first, right_env, right_other), jnp.where(first, right_other, right_env)],
        axis=0,
    )
    return apply(places, pairs, core_word, got, others, right, theta_blocks.dtype)


def solution(mesh):
    return jax.shard_map(
        on_device,
        mesh=mesh,
        in_specs=(
            P("sec"),
            P("sec"),
            P("sec"),
            P("sec", "mpo"),
            P("sec", None, None),
            P("sec", "mpo", None, None),
            P("mpo", None, None),
        ),
        out_specs=P("mpo", "sec", None),
        check_vma=False,
    )
```

```python
import functools

import jax
import jax.numpy as jnp
from jax import lax
from jax.experimental import pallas as pl
from jax.experimental.pallas import tpu as pltpu
from jax.sharding import PartitionSpec as P

SWAP = [(0, 1), (1, 0)]
TAIL = 8
GROUP = 16
STEP = 8
LANES = 128
HBM = pl.BlockSpec(memory_space=pltpu.HBM)


def copy(source, target, sem):
    return pltpu.make_async_copy(source, target, sem)


def pack_kernel(
    owner_ref, slot_ref, dims_ref, core_ref, theta_ref, left_ref, out_ref,
    left, theta, notes, blank, load_sems, store_sems, blank_sem,
):
    slots, channels, _, half, cols = left_ref.shape
    quarter = half // 2
    bulk = channels * half
    sides = cols // LANES
    body = sides * (bulk + quarter)
    core = core_ref[0]

    def load(i, carry):
        copy(left_ref.at[i], left.at[i], load_sems.at[0, i]).start()
        copy(theta_ref.at[i, :, core], theta.at[i], load_sems.at[1, i]).start()
        return carry

    lax.fori_loop(0, slots, load, 0)

    blank[...] = jnp.zeros_like(blank)
    clear = copy(blank, out_ref.at[:, pl.ds(body, TAIL)], blank_sem)
    clear.start()
    clear.wait()
    tail_rows = lax.broadcasted_iota(jnp.int32, (2, TAIL, LANES), 1)

    def store(i, carry):
        text = jnp.where(tail_rows == 0, slot_ref[i] + 1, dims_ref[i])
        notes[i] = text.astype(jnp.float32).astype(notes.dtype)
        place = 2 * owner_ref[i]
        pair = pl.ds(place, 2)
        copy(notes.at[i], out_ref.at[pair, pl.ds(body, TAIL)], store_sems.at[i]).start()
        copy(left_ref.at[i], left.at[i], load_sems.at[0, i]).wait()
        for c in range(sides):
            lanes = pl.ds(c * LANES, LANES)
            for h in range(2):
                copy(
                    left.at[i, :, h, :, lanes],
                    out_ref.at[place + h, pl.ds(c * bulk, bulk)].reshape(
                        channels, half, LANES
                    ),
                    store_sems.at[i],
                ).start()
        copy(theta_ref.at[i, :, core], theta.at[i], load_sems.at[1, i]).wait()
        for c in range(sides):
            copy(
                theta.at[i, :, :, pl.ds(c * LANES, LANES)],
                out_ref.at[pair, pl.ds(sides * bulk + c * quarter, quarter)],
                store_sems.at[i],
            ).start()
        return carry

    lax.fori_loop(0, slots, store, 0)

    def settle(i, carry):
        pair = out_ref.at[pl.ds(2 * owner_ref[i], 2)]
        copy(pair, pair, store_sems.at[i]).wait()
        return carry

    lax.fori_loop(0, slots, settle, 0)


def pack(new_owner, new_slot, sector_dims, core, theta_blocks, left_env, peers):
    slots, channels, tile, cols = left_env.shape
    half, quarter = tile // 2, tile // 4
    rows = (cols // LANES) * (channels * half + quarter) + TAIL
    dtype = theta_blocks.dtype
    moved = 2 * slots * 2 * rows * LANES * 2
    return pl.pallas_call(
        pack_kernel,
        grid_spec=pltpu.PrefetchScalarGridSpec(
            num_scalar_prefetch=4,
            grid=(),
            in_specs=[HBM] * 2,
            out_specs=HBM,
            scratch_shapes=[
                pltpu.VMEM((slots, channels, 2, half, cols), dtype),
                pltpu.VMEM((slots, 2, quarter, cols), dtype),
                pltpu.VMEM((slots, 2, TAIL, LANES), dtype),
                pltpu.VMEM((2 * peers, TAIL, LANES), dtype),
                pltpu.SemaphoreType.DMA((2, slots)),
                pltpu.SemaphoreType.DMA((slots,)),
                pltpu.SemaphoreType.DMA,
            ],
        ),
        out_shape=jax.ShapeDtypeStruct((2 * peers, rows, LANES), dtype),
        compiler_params=pltpu.CompilerParams(vmem_limit_bytes=60 << 20),
        cost_estimate=pl.CostEstimate(flops=0, bytes_accessed=moved, transcendentals=0),
        name="pack_parcels",
    )(
        new_owner, new_slot, sector_dims, core,
        theta_blocks.reshape(slots, 2, 2, quarter, cols),
        left_env.reshape(slots, channels, 2, half, cols),
    )


def split_kernel(first, got_ref, *refs):
    outs_ref, sems = refs[:-1], refs[-1]
    quarter = outs_ref[0].shape[1]
    moves = [
        copy(got_ref.at[:, pl.ds(first + c * quarter, quarter)], out_ref, sems.at[c])
        for c, out_ref in enumerate(outs_ref)
    ]
    for move in moves:
        move.start()
    for move in moves:
        move.wait()


def split(got, first, quarter, sides):
    parcels = got.shape[0]
    part = jax.ShapeDtypeStruct((parcels, quarter, LANES), got.dtype)
    return pl.pallas_call(
        functools.partial(split_kernel, first),
        in_specs=[HBM],
        out_specs=[pl.BlockSpec(memory_space=pltpu.VMEM)] * sides,
        scratch_shapes=[pltpu.SemaphoreType.DMA((sides,))],
        out_shape=[part] * sides,
        compiler_params=pltpu.CompilerParams(vmem_limit_bytes=44 << 20),
        cost_estimate=pl.CostEstimate(flops=0, bytes_accessed=8 << 20, transcendentals=0),
        name="theta_quarters",
    )(got)


def places_kernel(got_ref, out_ref, notes, note_sem):
    tails = copy(got_ref.at[:, pl.ds(got_ref.shape[1] - TAIL, TAIL)], notes, note_sem)
    tails.start()
    tails.wait()
    tail = notes[...].astype(jnp.float32)
    row = lax.broadcasted_iota(jnp.int32, tail.shape, 1)
    slot = jnp.sum(jnp.where(row == 0, tail, 0.0), axis=1)
    live = jnp.sum(jnp.where(row == 1, tail, 0.0), axis=1)
    parcel = lax.broadcasted_iota(jnp.int32, slot.shape, 0)
    wanted = lax.broadcasted_iota(jnp.int32, slot.shape, 1) + 1
    lands = (slot.astype(jnp.int32) == wanted) & (parcel % 2 == 0)
    anchor = jnp.sum(jnp.where(lands, parcel, 0), axis=0, keepdims=True)
    dims = jnp.sum(jnp.where(lands, live.astype(jnp.int32), 0), axis=0, keepdims=True)
    out_ref[0:1, :] = anchor
    out_ref[1:2, :] = dims


def find_places(got):
    parcels = got.shape[0]
    return pl.pallas_call(
        places_kernel,
        in_specs=[HBM],
        out_specs=pl.BlockSpec(memory_space=pltpu.VMEM),
        scratch_shapes=[
            pltpu.VMEM((parcels, TAIL, LANES), got.dtype),
            pltpu.SemaphoreType.DMA,
        ],
        out_shape=jax.ShapeDtypeStruct((2, LANES), jnp.int32),
        compiler_params=pltpu.CompilerParams(vmem_limit_bytes=60 << 20),
        cost_estimate=pl.CostEstimate(flops=0, bytes_accessed=8 << 20, transcendentals=0),
        name="places",
    )(got)


def apply_kernel(sides, places_ref, pairs_ref, core_ref, got_ref, *refs):
    others_ref, right_ref, out_ref = refs[:sides], refs[sides], refs[sides + 1]
    theta, left, inner, even, odd, turned, theta_sems, left_sems, out_sems = refs[sides + 2:]
    slots, _, _, quarter, cols = theta.shape
    half, tile, bulk = 2 * quarter, 4 * quarter, left.shape[2]
    channels = 2 * bulk // half
    core = core_ref[0]
    groups, steps = slots // GROUP, GROUP // STEP
    part = half // steps

    def fetch(j, carry):
        pair = pl.ds(places_ref[0, j], 2)
        for c in range(sides):
            lanes = pl.ds(c * LANES, LANES)
            copy(
                got_ref.at[pair, pl.ds(sides * bulk + c * quarter, quarter)],
                theta.at[j, core, :, :, lanes],
                theta_sems.at[j],
            ).start()
            copy(
                others_ref[c].at[pair], theta.at[j, 1 - core, :, :, lanes], theta_sems.at[j]
            ).start()
        return carry

    lax.fori_loop(0, slots, fetch, 0)

    strip = 16
    strip_rows = lax.broadcasted_iota(jnp.int32, (strip, cols), 0)

    def trim(j, carry):
        for c in range(sides):
            copy(
                got_ref.at[pl.ds(places_ref[0, j], 2), pl.ds(c * bulk, bulk)],
                left.at[j, :, :, pl.ds(c * LANES, LANES)],
                left_sems.at[j],
            ).start()
        copy(theta.at[j], theta.at[j], theta_sems.at[j]).wait()
        live = places_ref[1, j]

        block = theta.at[j].reshape(tile, cols)

        def clear(t, inner_carry):
            first = pl.multiple_of(t * strip, strip)
            rows = block[pl.ds(first, strip)].astype(jnp.float32)
            rows = jnp.where(strip_rows + first < live, rows, 0.0)
            block[pl.ds(first, strip)] = rows.astype(theta.dtype)
            return inner_carry

        return lax.fori_loop(live // strip, tile // strip, clear, carry)

    lax.fori_loop(0, slots, trim, 0)

    half_ids = lax.broadcasted_iota(jnp.int32, (half, cols), 0) + core * half

    def turn(g, b):
        first = pl.multiple_of(b * part, part)
        rows = (even, odd)[g % 2][:, pl.ds(first, part), :]
        turned[g, pl.ds(first, part)] = pltpu.einshape("krn->rkn", rows).astype(turned.dtype)

    def write(g):
        return copy(turned.at[g], out_ref.at[:, pl.ds(g * GROUP, GROUP)], out_sems.at[g])

    for g in range(groups):

        def contract(b, carry):
            for k in range(STEP):
                j = g * GROUP + b * STEP + k
                copy(left.at[j], left.at[j], left_sems.at[j]).wait()
            for k in range(STEP):
                j = g * GROUP + b * STEP + k
                for w in range(channels):
                    inner[k * half:(k + 1) * half, w * cols:(w + 1) * cols] = jnp.dot(
                        left[j, w // 2, pl.ds(w % 2 * half, half)],
                        theta[pairs_ref[w, j]].reshape(tile, cols),
                        preferred_element_type=jnp.float32,
                    ).astype(inner.dtype)
            if g > 0:
                turn(g - 1, b)
            total = jnp.dot(
                inner[...], right_ref[...], preferred_element_type=jnp.float32
            )
            for k in range(STEP):
                live = places_ref[1, g * GROUP + b * STEP + k]
                (even, odd)[g % 2][b * STEP + k] = jnp.where(
                    half_ids < live, total[k * half:(k + 1) * half], 0.0
                )
            return carry

        lax.fori_loop(0, steps, contract, 0)
        if g > 0:
            write(g - 1).start()

    for b in range(steps):
        turn(groups - 1, b)
    write(groups - 1).start()
    for g in range(groups):
        write(g).wait()


def apply(places, pairs, core, got, others, right, dtype):
    channels, tile, cols = right.shape
    slots = pairs.shape[1]
    half, quarter = tile // 2, tile // 4
    flops = 4 * slots * channels * half * tile * cols
    moved = 2 * slots * cols * (tile + channels * half + half)
    return pl.pallas_call(
        functools.partial(apply_kernel, cols // LANES),
        grid_spec=pltpu.PrefetchScalarGridSpec(
            num_scalar_prefetch=3,
            grid=(),
            in_specs=[HBM] * (1 + len(others)) + [pl.BlockSpec(memory_space=pltpu.VMEM)],
            out_specs=HBM,
            scratch_shapes=[
                pltpu.VMEM((slots, 2, 2, quarter, cols), dtype),
                pltpu.VMEM((slots, 2, channels * half // 2, cols), dtype),
                pltpu.VMEM((STEP * half, channels * cols), dtype),
                pltpu.VMEM((GROUP, half, cols), jnp.float32),
                pltpu.VMEM((GROUP, half, cols), jnp.float32),
                pltpu.VMEM((slots // GROUP, half, GROUP, cols), dtype),
                pltpu.SemaphoreType.DMA((slots,)),
                pltpu.SemaphoreType.DMA((slots,)),
                pltpu.SemaphoreType.DMA((slots // GROUP,)),
            ],
        ),
        out_shape=jax.ShapeDtypeStruct((half, slots, cols), dtype),
        compiler_params=pltpu.CompilerParams(vmem_limit_bytes=60 << 20),
        cost_estimate=pl.CostEstimate(flops=flops, bytes_accessed=moved, transcendentals=0),
        name="contract",
    )(places, pairs, core, got, *others, right.reshape(channels * tile, cols))


def on_device(sector_dims, new_owner, new_slot, block_pairs, theta_blocks, left_env, right_env):
    peers = lax.axis_size("sec")
    core = lax.axis_index("mpo")
    core_word = core.astype(jnp.int32).reshape(1)

    right_other = lax.ppermute(right_env, "mpo", SWAP)
    pairs_other = lax.ppermute(block_pairs, "mpo", SWAP)
    parcels = pack(
        new_owner, new_slot, sector_dims, core_word, theta_blocks, left_env, peers
    )
    parcels, right_other, pairs_other = lax.optimization_barrier(
        (parcels, right_other, pairs_other)
    )
    got = lax.all_to_all(parcels, ("sec", "mpo"), split_axis=0, concat_axis=0, tiled=True)
    got, right_other, pairs_other, core = lax.optimization_barrier(
        (got, right_other, pairs_other, core)
    )
    channels, tile, cols = left_env.shape[1:]
    bulk = (cols // LANES) * channels * tile // 2
    others = [
        lax.ppermute(quarters, "mpo", SWAP)
        for quarters in split(got, bulk, tile // 4, cols // LANES)
    ]
    places = find_places(got)
    first = core == 0
    pairs = jnp.concatenate(
        [jnp.where(first, block_pairs, pairs_other), jnp.where(first, pairs_other, block_pairs)],
        axis=1,
    ).T
    right = jnp.concatenate(
        [jnp.where(first, right_env, right_other), jnp.where(first, right_other, right_env)],
        axis=0,
    )
    return apply(places, pairs, core_word, got, others, right, theta_blocks.dtype)


def solution(mesh):
    return jax.shard_map(
        on_device,
        mesh=mesh,
        in_specs=(
            P("sec"),
            P("sec"),
            P("sec"),
            P("sec", "mpo"),
            P("sec", None, None),
            P("sec", "mpo", None, None),
            P("mpo", None, None),
        ),
        out_specs=P("mpo", "sec", None),
        check_vma=False,
    )
```

```python
import functools

import jax
import jax.numpy as jnp
from jax import lax
from jax.experimental import pallas as pl
from jax.experimental.pallas import tpu as pltpu
from jax.sharding import PartitionSpec as P

SWAP = [(0, 1), (1, 0)]
TAIL = 8
GROUP = 16
STEP = 8
LANES = 128
HBM = pl.BlockSpec(memory_space=pltpu.HBM)


def copy(source, target, sem):
    return pltpu.make_async_copy(source, target, sem)


def pack_kernel(
    owner_ref, slot_ref, dims_ref, core_ref, theta_ref, left_ref, out_ref,
    left, theta, notes, blank, load_sems, store_sems, blank_sem,
):
    slots, channels, _, half, cols = left_ref.shape
    quarter = half // 2
    bulk = channels * half
    sides = cols // LANES
    body = sides * (bulk + quarter)
    core = core_ref[0]

    def load(i, carry):
        copy(left_ref.at[i], left.at[i], load_sems.at[0, i]).start()
        copy(theta_ref.at[i, :, core], theta.at[i], load_sems.at[1, i]).start()
        return carry

    lax.fori_loop(0, slots, load, 0)

    blank[...] = jnp.zeros_like(blank)
    clear = copy(blank, out_ref.at[:, pl.ds(body, TAIL)], blank_sem)
    clear.start()
    clear.wait()
    tail_rows = lax.broadcasted_iota(jnp.int32, (2, TAIL, LANES), 1)

    def store(i, carry):
        text = jnp.where(tail_rows == 0, slot_ref[i] + 1, dims_ref[i])
        notes[i] = text.astype(jnp.float32).astype(notes.dtype)
        place = 2 * owner_ref[i]
        pair = pl.ds(place, 2)
        copy(notes.at[i], out_ref.at[pair, pl.ds(body, TAIL)], store_sems.at[i]).start()
        copy(left_ref.at[i], left.at[i], load_sems.at[0, i]).wait()
        for c in range(sides):
            lanes = pl.ds(c * LANES, LANES)
            for h in range(2):
                copy(
                    left.at[i, :, h, :, lanes],
                    out_ref.at[place + h, pl.ds(c * bulk, bulk)].reshape(
                        channels, half, LANES
                    ),
                    store_sems.at[i],
                ).start()
        copy(theta_ref.at[i, :, core], theta.at[i], load_sems.at[1, i]).wait()
        for c in range(sides):
            copy(
                theta.at[i, :, :, pl.ds(c * LANES, LANES)],
                out_ref.at[pair, pl.ds(sides * bulk + c * quarter, quarter)],
                store_sems.at[i],
            ).start()
        return carry

    lax.fori_loop(0, slots, store, 0)

    def settle(i, carry):
        pair = out_ref.at[pl.ds(2 * owner_ref[i], 2)]
        copy(pair, pair, store_sems.at[i]).wait()
        return carry

    lax.fori_loop(0, slots, settle, 0)


def pack(new_owner, new_slot, sector_dims, core, theta_blocks, left_env, peers):
    slots, channels, tile, cols = left_env.shape
    half, quarter = tile // 2, tile // 4
    rows = (cols // LANES) * (channels * half + quarter) + TAIL
    dtype = theta_blocks.dtype
    moved = 2 * slots * 2 * rows * LANES * 2
    return pl.pallas_call(
        pack_kernel,
        grid_spec=pltpu.PrefetchScalarGridSpec(
            num_scalar_prefetch=4,
            grid=(),
            in_specs=[HBM] * 2,
            out_specs=HBM,
            scratch_shapes=[
                pltpu.VMEM((slots, channels, 2, half, cols), dtype),
                pltpu.VMEM((slots, 2, quarter, cols), dtype),
                pltpu.VMEM((slots, 2, TAIL, LANES), dtype),
                pltpu.VMEM((2 * peers, TAIL, LANES), dtype),
                pltpu.SemaphoreType.DMA((2, slots)),
                pltpu.SemaphoreType.DMA((slots,)),
                pltpu.SemaphoreType.DMA,
            ],
        ),
        out_shape=jax.ShapeDtypeStruct((2 * peers, rows, LANES), dtype),
        compiler_params=pltpu.CompilerParams(vmem_limit_bytes=60 << 20),
        cost_estimate=pl.CostEstimate(flops=0, bytes_accessed=moved, transcendentals=0),
        name="pack_parcels",
    )(
        new_owner, new_slot, sector_dims, core,
        theta_blocks.reshape(slots, 2, 2, quarter, cols),
        left_env.reshape(slots, channels, 2, half, cols),
    )


def split_kernel(first, got_ref, *refs):
    outs_ref, sems = refs[:-1], refs[-1]
    quarter = outs_ref[0].shape[1]
    moves = [
        copy(got_ref.at[:, pl.ds(first + c * quarter, quarter)], out_ref, sems.at[c])
        for c, out_ref in enumerate(outs_ref)
    ]
    for move in moves:
        move.start()
    for move in moves:
        move.wait()


def split(got, first, quarter, sides):
    parcels = got.shape[0]
    part = jax.ShapeDtypeStruct((parcels, quarter, LANES), got.dtype)
    return pl.pallas_call(
        functools.partial(split_kernel, first),
        in_specs=[HBM],
        out_specs=[pl.BlockSpec(memory_space=pltpu.VMEM)] * sides,
        scratch_shapes=[pltpu.SemaphoreType.DMA((sides,))],
        out_shape=[part] * sides,
        compiler_params=pltpu.CompilerParams(vmem_limit_bytes=44 << 20),
        cost_estimate=pl.CostEstimate(flops=0, bytes_accessed=8 << 20, transcendentals=0),
        name="theta_quarters",
    )(got)


def places_kernel(got_ref, out_ref, notes, note_sem):
    tails = copy(got_ref.at[:, pl.ds(got_ref.shape[1] - TAIL, TAIL)], notes, note_sem)
    tails.start()
    tails.wait()
    tail = notes[...].astype(jnp.float32)
    row = lax.broadcasted_iota(jnp.int32, tail.shape, 1)
    slot = jnp.sum(jnp.where(row == 0, tail, 0.0), axis=1)
    live = jnp.sum(jnp.where(row == 1, tail, 0.0), axis=1)
    parcel = lax.broadcasted_iota(jnp.int32, slot.shape, 0)
    wanted = lax.broadcasted_iota(jnp.int32, slot.shape, 1) + 1
    lands = (slot.astype(jnp.int32) == wanted) & (parcel % 2 == 0)
    anchor = jnp.sum(jnp.where(lands, parcel, 0), axis=0, keepdims=True)
    dims = jnp.sum(jnp.where(lands, live.astype(jnp.int32), 0), axis=0, keepdims=True)
    out_ref[0:1, :] = anchor
    out_ref[1:2, :] = dims


def find_places(got):
    parcels = got.shape[0]
    return pl.pallas_call(
        places_kernel,
        in_specs=[HBM],
        out_specs=pl.BlockSpec(memory_space=pltpu.VMEM),
        scratch_shapes=[
            pltpu.VMEM((parcels, TAIL, LANES), got.dtype),
            pltpu.SemaphoreType.DMA,
        ],
        out_shape=jax.ShapeDtypeStruct((2, LANES), jnp.int32),
        compiler_params=pltpu.CompilerParams(vmem_limit_bytes=60 << 20),
        cost_estimate=pl.CostEstimate(flops=0, bytes_accessed=8 << 20, transcendentals=0),
        name="places",
    )(got)


def apply_kernel(sides, places_ref, pairs_ref, core_ref, got_ref, *refs):
    others_ref, right_hbm, out_ref = refs[:sides], refs[sides], refs[sides + 1]
    theta, left, inner, even, odd, turned, right_ref = refs[sides + 2:sides + 9]
    theta_sems, left_sems, out_sems, right_sem = refs[sides + 9:]
    slots, _, _, quarter, cols = theta.shape
    half, tile, bulk = 2 * quarter, 4 * quarter, left.shape[2]
    channels = 2 * bulk // half
    core = core_ref[0]
    groups, steps = slots // GROUP, GROUP // STEP
    part = half // steps

    def fetch(j, carry):
        pair = pl.ds(places_ref[0, j], 2)
        for c in range(sides):
            lanes = pl.ds(c * LANES, LANES)
            copy(
                got_ref.at[pair, pl.ds(sides * bulk + c * quarter, quarter)],
                theta.at[j, core, :, :, lanes],
                theta_sems.at[j],
            ).start()
            copy(
                others_ref[c].at[pair], theta.at[j, 1 - core, :, :, lanes], theta_sems.at[j]
            ).start()
        return carry

    lax.fori_loop(0, slots, fetch, 0)
    fetch_right = copy(right_hbm, right_ref, right_sem)
    fetch_right.start()

    strip = 16
    strip_rows = lax.broadcasted_iota(jnp.int32, (strip, cols), 0)

    def trim(j, carry):
        for c in range(sides):
            copy(
                got_ref.at[pl.ds(places_ref[0, j], 2), pl.ds(c * bulk, bulk)],
                left.at[j, :, :, pl.ds(c * LANES, LANES)],
                left_sems.at[j],
            ).start()
        copy(theta.at[j], theta.at[j], theta_sems.at[j]).wait()
        live = places_ref[1, j]

        block = theta.at[j].reshape(tile, cols)

        def clear(t, inner_carry):
            first = pl.multiple_of(t * strip, strip)
            rows = block[pl.ds(first, strip)].astype(jnp.float32)
            rows = jnp.where(strip_rows + first < live, rows, 0.0)
            block[pl.ds(first, strip)] = rows.astype(theta.dtype)
            return inner_carry

        return lax.fori_loop(live // strip, tile // strip, clear, carry)

    lax.fori_loop(0, slots, trim, 0)
    fetch_right.wait()

    half_ids = lax.broadcasted_iota(jnp.int32, (half, cols), 0) + core * half

    def turn(g, b):
        first = pl.multiple_of(b * part, part)
        rows = (even, odd)[g % 2][:, pl.ds(first, part), :]
        turned[g, pl.ds(first, part)] = pltpu.einshape("krn->rkn", rows).astype(turned.dtype)

    def write(g):
        return copy(turned.at[g], out_ref.at[:, pl.ds(g * GROUP, GROUP)], out_sems.at[g])

    for g in range(groups):

        def contract(b, carry):
            for k in range(STEP):
                j = g * GROUP + b * STEP + k
                copy(left.at[j], left.at[j], left_sems.at[j]).wait()
            for k in range(STEP):
                j = g * GROUP + b * STEP + k
                for w in range(channels):
                    inner[k * half:(k + 1) * half, w * cols:(w + 1) * cols] = jnp.dot(
                        left[j, w // 2, pl.ds(w % 2 * half, half)],
                        theta[pairs_ref[w, j]].reshape(tile, cols),
                        preferred_element_type=jnp.float32,
                    ).astype(inner.dtype)
            if g > 0:
                turn(g - 1, b)
            total = jnp.dot(
                inner[...], right_ref[...], preferred_element_type=jnp.float32
            )
            for k in range(STEP):
                live = places_ref[1, g * GROUP + b * STEP + k]
                (even, odd)[g % 2][b * STEP + k] = jnp.where(
                    half_ids < live, total[k * half:(k + 1) * half], 0.0
                )
            return carry

        lax.fori_loop(0, steps, contract, 0)
        if g > 0:
            write(g - 1).start()

    for b in range(steps):
        turn(groups - 1, b)
    write(groups - 1).start()
    for g in range(groups):
        write(g).wait()


def apply(places, pairs, core, got, others, right, dtype):
    channels, tile, cols = right.shape
    slots = pairs.shape[1]
    half, quarter = tile // 2, tile // 4
    flops = 4 * slots * channels * half * tile * cols
    moved = 2 * slots * cols * (tile + channels * half + half)
    return pl.pallas_call(
        functools.partial(apply_kernel, cols // LANES),
        grid_spec=pltpu.PrefetchScalarGridSpec(
            num_scalar_prefetch=3,
            grid=(),
            in_specs=[HBM] * (2 + len(others)),
            out_specs=HBM,
            scratch_shapes=[
                pltpu.VMEM((slots, 2, 2, quarter, cols), dtype),
                pltpu.VMEM((slots, 2, channels * half // 2, cols), dtype),
                pltpu.VMEM((STEP * half, channels * cols), dtype),
                pltpu.VMEM((GROUP, half, cols), jnp.float32),
                pltpu.VMEM((GROUP, half, cols), jnp.float32),
                pltpu.VMEM((slots // GROUP, half, GROUP, cols), dtype),
                pltpu.VMEM((channels * tile, cols), dtype),
                pltpu.SemaphoreType.DMA((slots,)),
                pltpu.SemaphoreType.DMA((slots,)),
                pltpu.SemaphoreType.DMA((slots // GROUP,)),
                pltpu.SemaphoreType.DMA,
            ],
        ),
        out_shape=jax.ShapeDtypeStruct((half, slots, cols), dtype),
        compiler_params=pltpu.CompilerParams(vmem_limit_bytes=60 << 20),
        cost_estimate=pl.CostEstimate(flops=flops, bytes_accessed=moved, transcendentals=0),
        name="contract",
    )(places, pairs, core, got, *others, right.reshape(channels * tile, cols))


def on_device(sector_dims, new_owner, new_slot, block_pairs, theta_blocks, left_env, right_env):
    peers = lax.axis_size("sec")
    core = lax.axis_index("mpo")
    core_word = core.astype(jnp.int32).reshape(1)

    right_other = lax.ppermute(right_env, "mpo", SWAP)
    pairs_other = lax.ppermute(block_pairs, "mpo", SWAP)
    parcels = pack(
        new_owner, new_slot, sector_dims, core_word, theta_blocks, left_env, peers
    )
    parcels, right_other, pairs_other = lax.optimization_barrier(
        (parcels, right_other, pairs_other)
    )
    got = lax.all_to_all(parcels, ("sec", "mpo"), split_axis=0, concat_axis=0, tiled=True)
    got, right_other, pairs_other, core = lax.optimization_barrier(
        (got, right_other, pairs_other, core)
    )
    channels, tile, cols = left_env.shape[1:]
    bulk = (cols // LANES) * channels * tile // 2
    others = [
        lax.ppermute(quarters, "mpo", SWAP)
        for quarters in split(got, bulk, tile // 4, cols // LANES)
    ]
    places = find_places(got)
    first = core == 0
    pairs = jnp.concatenate(
        [jnp.where(first, block_pairs, pairs_other), jnp.where(first, pairs_other, block_pairs)],
        axis=1,
    ).T
    right = jnp.concatenate(
        [jnp.where(first, right_env, right_other), jnp.where(first, right_other, right_env)],
        axis=0,
    )
    return apply(places, pairs, core_word, got, others, right, theta_blocks.dtype)


def solution(mesh):
    return jax.shard_map(
        on_device,
        mesh=mesh,
        in_specs=(
            P("sec"),
            P("sec"),
            P("sec"),
            P("sec", "mpo"),
            P("sec", None, None),
            P("sec", "mpo", None, None),
            P("mpo", None, None),
        ),
        out_specs=P("mpo", "sec", None),
        check_vma=False,
    )
```

```python
import functools

import jax
import jax.numpy as jnp
from jax import lax
from jax.experimental import pallas as pl
from jax.experimental.pallas import tpu as pltpu
from jax.sharding import PartitionSpec as P

SWAP = [(0, 1), (1, 0)]
TAIL = 8
GROUP = 16
STEP = 8
LANES = 128
HBM = pl.BlockSpec(memory_space=pltpu.HBM)


def copy(source, target, sem):
    return pltpu.make_async_copy(source, target, sem)


def pack_kernel(
    owner_ref, slot_ref, dims_ref, core_ref, theta_ref, left_ref, out_ref,
    left, theta, notes, blank, load_sems, store_sems, blank_sem,
):
    slots, channels, _, half, cols = left_ref.shape
    quarter = half // 2
    bulk = channels * half
    sides = cols // LANES
    body = sides * (bulk + quarter)
    core = core_ref[0]

    def load(i, carry):
        copy(left_ref.at[i], left.at[i], load_sems.at[0, i]).start()
        copy(theta_ref.at[i, :, core], theta.at[i], load_sems.at[1, i]).start()
        return carry

    lax.fori_loop(0, slots, load, 0)

    blank[...] = jnp.zeros_like(blank)
    clear = copy(blank, out_ref.at[:, pl.ds(body, TAIL)], blank_sem)
    clear.start()
    clear.wait()
    tail_rows = lax.broadcasted_iota(jnp.int32, (2, TAIL, LANES), 1)

    def store(i, carry):
        text = jnp.where(tail_rows == 0, slot_ref[i] + 1, dims_ref[i])
        notes[i] = text.astype(jnp.float32).astype(notes.dtype)
        place = 2 * owner_ref[i]
        pair = pl.ds(place, 2)
        copy(notes.at[i], out_ref.at[pair, pl.ds(body, TAIL)], store_sems.at[i]).start()
        copy(left_ref.at[i], left.at[i], load_sems.at[0, i]).wait()
        for c in range(sides):
            lanes = pl.ds(c * LANES, LANES)
            for h in range(2):
                copy(
                    left.at[i, :, h, :, lanes],
                    out_ref.at[place + h, pl.ds(c * bulk, bulk)].reshape(
                        channels, half, LANES
                    ),
                    store_sems.at[i],
                ).start()
        copy(theta_ref.at[i, :, core], theta.at[i], load_sems.at[1, i]).wait()
        for c in range(sides):
            copy(
                theta.at[i, :, :, pl.ds(c * LANES, LANES)],
                out_ref.at[pair, pl.ds(sides * bulk + c * quarter, quarter)],
                store_sems.at[i],
            ).start()
        return carry

    lax.fori_loop(0, slots, store, 0)

    def settle(i, carry):
        pair = out_ref.at[pl.ds(2 * owner_ref[i], 2)]
        copy(pair, pair, store_sems.at[i]).wait()
        return carry

    lax.fori_loop(0, slots, settle, 0)


def pack(new_owner, new_slot, sector_dims, core, theta_blocks, left_env, peers):
    slots, channels, tile, cols = left_env.shape
    half, quarter = tile // 2, tile // 4
    rows = (cols // LANES) * (channels * half + quarter) + TAIL
    dtype = theta_blocks.dtype
    moved = 2 * slots * 2 * rows * LANES * 2
    return pl.pallas_call(
        pack_kernel,
        grid_spec=pltpu.PrefetchScalarGridSpec(
            num_scalar_prefetch=4,
            grid=(),
            in_specs=[HBM] * 2,
            out_specs=HBM,
            scratch_shapes=[
                pltpu.VMEM((slots, channels, 2, half, cols), dtype),
                pltpu.VMEM((slots, 2, quarter, cols), dtype),
                pltpu.VMEM((slots, 2, TAIL, LANES), dtype),
                pltpu.VMEM((2 * peers, TAIL, LANES), dtype),
                pltpu.SemaphoreType.DMA((2, slots)),
                pltpu.SemaphoreType.DMA((slots,)),
                pltpu.SemaphoreType.DMA,
            ],
        ),
        out_shape=jax.ShapeDtypeStruct((2 * peers, rows, LANES), dtype),
        compiler_params=pltpu.CompilerParams(vmem_limit_bytes=60 << 20),
        cost_estimate=pl.CostEstimate(flops=0, bytes_accessed=moved, transcendentals=0),
        name="pack_parcels",
    )(
        new_owner, new_slot, sector_dims, core,
        theta_blocks.reshape(slots, 2, 2, quarter, cols),
        left_env.reshape(slots, channels, 2, half, cols),
    )


def split_kernel(first, got_ref, *refs):
    outs_ref, (staged, read_sems, write_sems) = refs[:-3], refs[-3:]
    quarter = outs_ref[0].shape[1]
    parts = read_sems.shape[0]
    size = staged.shape[0] // parts
    spans = [pl.ds(p * size, size) for p in range(parts)]
    reads = [
        copy(got_ref.at[span, pl.ds(first, staged.shape[1])], staged.at[span], read_sems.at[p])
        for p, span in enumerate(spans)
    ]
    writes = [
        copy(
            staged.at[span, pl.ds(c * quarter, quarter)],
            out_ref.at[span],
            write_sems.at[p, c],
        )
        for p, span in enumerate(spans)
        for c, out_ref in enumerate(outs_ref)
    ]
    for read in reads:
        read.start()
    for p in range(parts):
        reads[p].wait()
        for c in range(len(outs_ref)):
            writes[p * len(outs_ref) + c].start()
    for write in writes:
        write.wait()


def split(got, first, quarter, sides):
    parcels = got.shape[0]
    part = jax.ShapeDtypeStruct((parcels, quarter, LANES), got.dtype)
    return pl.pallas_call(
        functools.partial(split_kernel, first),
        in_specs=[HBM],
        out_specs=[HBM] * sides,
        scratch_shapes=[
            pltpu.VMEM((parcels, sides * quarter, LANES), got.dtype),
            pltpu.SemaphoreType.DMA((8,)),
            pltpu.SemaphoreType.DMA((8, sides)),
        ],
        out_shape=[part] * sides,
        compiler_params=pltpu.CompilerParams(vmem_limit_bytes=60 << 20),
        cost_estimate=pl.CostEstimate(flops=0, bytes_accessed=8 << 20, transcendentals=0),
        name="theta_quarters",
    )(got)


def places_kernel(got_ref, out_ref, notes, note_sem):
    tails = copy(got_ref.at[:, pl.ds(got_ref.shape[1] - TAIL, TAIL)], notes, note_sem)
    tails.start()
    tails.wait()
    tail = notes[...].astype(jnp.float32)
    row = lax.broadcasted_iota(jnp.int32, tail.shape, 1)
    slot = jnp.sum(jnp.where(row == 0, tail, 0.0), axis=1)
    live = jnp.sum(jnp.where(row == 1, tail, 0.0), axis=1)
    parcel = lax.broadcasted_iota(jnp.int32, slot.shape, 0)
    wanted = lax.broadcasted_iota(jnp.int32, slot.shape, 1) + 1
    lands = (slot.astype(jnp.int32) == wanted) & (parcel % 2 == 0)
    anchor = jnp.sum(jnp.where(lands, parcel, 0), axis=0, keepdims=True)
    dims = jnp.sum(jnp.where(lands, live.astype(jnp.int32), 0), axis=0, keepdims=True)
    out_ref[0:1, :] = anchor
    out_ref[1:2, :] = dims


def find_places(got):
    parcels = got.shape[0]
    return pl.pallas_call(
        places_kernel,
        in_specs=[HBM],
        out_specs=pl.BlockSpec(memory_space=pltpu.VMEM),
        scratch_shapes=[
            pltpu.VMEM((parcels, TAIL, LANES), got.dtype),
            pltpu.SemaphoreType.DMA,
        ],
        out_shape=jax.ShapeDtypeStruct((2, LANES), jnp.int32),
        compiler_params=pltpu.CompilerParams(vmem_limit_bytes=60 << 20),
        cost_estimate=pl.CostEstimate(flops=0, bytes_accessed=8 << 20, transcendentals=0),
        name="places",
    )(got)


def apply_kernel(sides, places_ref, pairs_ref, core_ref, got_ref, *refs):
    others_ref, right_hbm, out_ref = refs[:sides], refs[sides], refs[sides + 1]
    theta, left, inner, even, odd, turned, right_ref = refs[sides + 2:sides + 9]
    theta_sems, left_sems, out_sems, right_sem = refs[sides + 9:]
    slots, _, _, quarter, cols = theta.shape
    half, tile, bulk = 2 * quarter, 4 * quarter, left.shape[2]
    channels = 2 * bulk // half
    core = core_ref[0]
    groups, steps = slots // GROUP, GROUP // STEP
    part = half // steps

    def fetch(j, carry):
        pair = pl.ds(places_ref[0, j], 2)
        for c in range(sides):
            lanes = pl.ds(c * LANES, LANES)
            copy(
                got_ref.at[pair, pl.ds(sides * bulk + c * quarter, quarter)],
                theta.at[j, core, :, :, lanes],
                theta_sems.at[j],
            ).start()
            copy(
                others_ref[c].at[pair], theta.at[j, 1 - core, :, :, lanes], theta_sems.at[j]
            ).start()
        return carry

    lax.fori_loop(0, slots, fetch, 0)
    fetch_right = copy(right_hbm, right_ref, right_sem)
    fetch_right.start()

    strip = 16
    strip_rows = lax.broadcasted_iota(jnp.int32, (strip, cols), 0)

    def trim(j, carry):
        for c in range(sides):
            copy(
                got_ref.at[pl.ds(places_ref[0, j], 2), pl.ds(c * bulk, bulk)],
                left.at[j, :, :, pl.ds(c * LANES, LANES)],
                left_sems.at[j],
            ).start()
        copy(theta.at[j], theta.at[j], theta_sems.at[j]).wait()
        live = places_ref[1, j]

        block = theta.at[j].reshape(tile, cols)

        def clear(t, inner_carry):
            first = pl.multiple_of(t * strip, strip)
            rows = block[pl.ds(first, strip)].astype(jnp.float32)
            rows = jnp.where(strip_rows + first < live, rows, 0.0)
            block[pl.ds(first, strip)] = rows.astype(theta.dtype)
            return inner_carry

        return lax.fori_loop(live // strip, tile // strip, clear, carry)

    lax.fori_loop(0, slots, trim, 0)
    fetch_right.wait()

    half_ids = lax.broadcasted_iota(jnp.int32, (half, cols), 0) + core * half

    def turn(g, b):
        first = pl.multiple_of(b * part, part)
        rows = (even, odd)[g % 2][:, pl.ds(first, part), :]
        turned[g, pl.ds(first, part)] = pltpu.einshape("krn->rkn", rows).astype(turned.dtype)

    def write(g):
        return copy(turned.at[g], out_ref.at[:, pl.ds(g * GROUP, GROUP)], out_sems.at[g])

    for g in range(groups):

        def contract(b, carry):
            for k in range(STEP):
                j = g * GROUP + b * STEP + k
                copy(left.at[j], left.at[j], left_sems.at[j]).wait()
            for k in range(STEP):
                j = g * GROUP + b * STEP + k
                for w in range(channels):
                    inner[k * half:(k + 1) * half, w * cols:(w + 1) * cols] = jnp.dot(
                        left[j, w // 2, pl.ds(w % 2 * half, half)],
                        theta[pairs_ref[w, j]].reshape(tile, cols),
                        preferred_element_type=jnp.float32,
                    ).astype(inner.dtype)
            if g > 0:
                turn(g - 1, b)
            total = jnp.dot(
                inner[...], right_ref[...], preferred_element_type=jnp.float32
            )
            for k in range(STEP):
                live = places_ref[1, g * GROUP + b * STEP + k]
                (even, odd)[g % 2][b * STEP + k] = jnp.where(
                    half_ids < live, total[k * half:(k + 1) * half], 0.0
                )
            return carry

        lax.fori_loop(0, steps, contract, 0)
        if g > 0:
            write(g - 1).start()

    def write_part(b):
        rows = pl.ds(b * part, part)
        return copy(
            turned.at[groups - 1, rows],
            out_ref.at[rows, pl.ds((groups - 1) * GROUP, GROUP)],
            out_sems.at[groups - 1 + b],
        )

    for b in range(steps):
        turn(groups - 1, b)
        write_part(b).start()
    for g in range(groups - 1):
        write(g).wait()
    for b in range(steps):
        write_part(b).wait()


def apply(places, pairs, core, got, others, right, dtype):
    channels, tile, cols = right.shape
    slots = pairs.shape[1]
    half, quarter = tile // 2, tile // 4
    flops = 4 * slots * channels * half * tile * cols
    moved = 2 * slots * cols * (tile + channels * half + half)
    return pl.pallas_call(
        functools.partial(apply_kernel, cols // LANES),
        grid_spec=pltpu.PrefetchScalarGridSpec(
            num_scalar_prefetch=3,
            grid=(),
            in_specs=[HBM] * (2 + len(others)),
            out_specs=HBM,
            scratch_shapes=[
                pltpu.VMEM((slots, 2, 2, quarter, cols), dtype),
                pltpu.VMEM((slots, 2, channels * half // 2, cols), dtype),
                pltpu.VMEM((STEP * half, channels * cols), dtype),
                pltpu.VMEM((GROUP, half, cols), jnp.float32),
                pltpu.VMEM((GROUP, half, cols), jnp.float32),
                pltpu.VMEM((slots // GROUP, half, GROUP, cols), dtype),
                pltpu.VMEM((channels * tile, cols), dtype),
                pltpu.SemaphoreType.DMA((slots,)),
                pltpu.SemaphoreType.DMA((slots,)),
                pltpu.SemaphoreType.DMA((slots // GROUP + GROUP // STEP - 1,)),
                pltpu.SemaphoreType.DMA,
            ],
        ),
        out_shape=jax.ShapeDtypeStruct((half, slots, cols), dtype),
        compiler_params=pltpu.CompilerParams(vmem_limit_bytes=60 << 20),
        cost_estimate=pl.CostEstimate(flops=flops, bytes_accessed=moved, transcendentals=0),
        name="contract",
    )(places, pairs, core, got, *others, right.reshape(channels * tile, cols))


def on_device(sector_dims, new_owner, new_slot, block_pairs, theta_blocks, left_env, right_env):
    peers = lax.axis_size("sec")
    core = lax.axis_index("mpo")
    core_word = core.astype(jnp.int32).reshape(1)

    right_other = lax.ppermute(right_env, "mpo", SWAP)
    pairs_other = lax.ppermute(block_pairs, "mpo", SWAP)
    parcels = pack(
        new_owner, new_slot, sector_dims, core_word, theta_blocks, left_env, peers
    )
    parcels, right_other, pairs_other = lax.optimization_barrier(
        (parcels, right_other, pairs_other)
    )
    got = lax.all_to_all(parcels, ("sec", "mpo"), split_axis=0, concat_axis=0, tiled=True)
    got, right_other, pairs_other, core = lax.optimization_barrier(
        (got, right_other, pairs_other, core)
    )
    channels, tile, cols = left_env.shape[1:]
    bulk = (cols // LANES) * channels * tile // 2
    others = [
        lax.ppermute(quarters, "mpo", SWAP)
        for quarters in split(got, bulk, tile // 4, cols // LANES)
    ]
    places = find_places(got)
    first = core == 0
    pairs = jnp.concatenate(
        [jnp.where(first, block_pairs, pairs_other), jnp.where(first, pairs_other, block_pairs)],
        axis=1,
    ).T
    right = jnp.concatenate(
        [jnp.where(first, right_env, right_other), jnp.where(first, right_other, right_env)],
        axis=0,
    )
    return apply(places, pairs, core_word, got, others, right, theta_blocks.dtype)


def solution(mesh):
    return jax.shard_map(
        on_device,
        mesh=mesh,
        in_specs=(
            P("sec"),
            P("sec"),
            P("sec"),
            P("sec", "mpo"),
            P("sec", None, None),
            P("sec", "mpo", None, None),
            P("mpo", None, None),
        ),
        out_specs=P("mpo", "sec", None),
        check_vma=False,
    )
```
